128 devices in a mesh: expert: 16 (over z, x), row: 8 (over y, core).
Axes of the slice: x: 4, y: 4, z: 4, core: 2. Of those that a mesh axis runs over, the one named last changes fastest.
Arguments:
- base_weights: bfloat16 [32, 2, 1536, 4096], P(None, None, 'row', 'expert'), may hold values from -6 to 6
- adapter_up_factor: bfloat16 [32, 2, 64, 1536], P(None, None, None, 'row'), may hold values from -6 to 6
- adapter_down: bfloat16 [32, 2, 64, 4096], P(None, None, 'row', 'expert'), may hold values from -6 to 6
- file_sizes: int32 [16], replicated, may hold values from 1 to 8, 64 in all
- file_writer: int32 [16], replicated, may hold values from 0 to 15, each once
Outputs:
- merged_store: bfloat16 [128, 1536, 4096], P('expert', 'row')
The draws below stay inside these ranges and needn't reach their ends.
Inputs may be any that keep to these rules, and one draw needn't show every extreme that they name: `file_sizes`: every file holds at least one tensor, together 2 * 32; the largest file holds exactly 8. `file_writer`: each rank along the expert axis owns exactly one file.
All inputs are finite; a program needn't handle non-finite values.
Results may differ from the reference program's by a relative error of at most 0.001.
Values may be sent and summed in bfloat16 or wider, within the bound.
No kernel may reach another device: no remote copies, remote signals or barrier semaphores. Data moves between devices by JAX's collectives and lax.ppermute only.
A program may use at most 192 MiB of HBM per device.

```python
import math
import jax
import jax.numpy as jnp
import numpy as np
from jax import lax

D = 4096
FF = 1536
R = 64
EXPERTS = 32
CAP = 8
N_EXPERT = 16


def steps_of(stream_key, extent, shards, low, high):
    factor_of = 1.0
    for axis_at, shards_of in shards:
        draws = jax.random.uniform(jax.random.fold_in(jax.random.fold_in(stream_key, 6), axis_at), (shards_of,), jnp.float32, low / len(shards), high / len(shards))
        factor_of = factor_of * jnp.repeat(jnp.exp(draws), extent[axis_at] // shards_of).reshape((-1,) + (1,) * (len(extent) - 1 - axis_at))
    return factor_of


def split_up(number_of, total, reach, slope):
    weights = [(1 << 20) // math.isqrt(rank ** slope) + 1 for rank in range(2, number_of + 1)]
    spare, holding = total - reach - (number_of - 1), [1] * (number_of - 1)
    while spare > 0:
        movable = [i for i in range(number_of - 1) if holding[i] < reach]
        pool, remaining = sum([weights[i] for i in movable]), spare
        for i in movable:
            more = min(reach - holding[i], max(1, remaining * weights[i] // pool), spare)
            holding[i] = holding[i] + more
            spare = spare - more
    return np.array([reach] + holding)


def ragged(stream_key, count, total, limit, lean):
    if count == 2:
        one = jax.random.randint(stream_key, (), max(1, total - limit), min(limit, total - 1) + 1)
        return jnp.stack([one, total - one])
    sizes = jnp.asarray(split_up(count, total, limit, lean), jnp.int32)
    pairs = (count - 1) // 2
    donor, receiver = sizes[1:1 + 2 * pairs:2], sizes[2:2 + 2 * pairs:2]
    room = jnp.minimum(donor - 1, limit - receiver)
    moved = jax.random.randint(jax.random.fold_in(stream_key, 1), (pairs,), 0, 1 << 20) % (room + 1)
    sizes = sizes.at[1:1 + 2 * pairs:2].set(donor - moved).at[2:2 + 2 * pairs:2].set(receiver + moved)
    return sizes[jax.random.permutation(jax.random.fold_in(stream_key, 2), count)]


def bell_draw(stream_key, extent, spread, limit, pieces=(), held_as=jnp.bfloat16):
    loudness = steps_of(stream_key, extent, pieces, -0.22, 0.18) if pieces else 1.0
    drawn = jax.random.normal(stream_key, extent, jnp.float32) * spread * loudness
    return jnp.minimum(jnp.maximum(drawn, -limit), limit).astype(held_as)


def setup_inputs(seed: int = 0) -> dict:
    seeds = jax.random.split(jax.random.key(seed), 6)
    base_weights = bell_draw(seeds[0], (EXPERTS, 2, FF, D), 1.0, 6.0, ((2, 8), (3, 16)))
    adapter_up_factor = bell_draw(seeds[1], (EXPERTS, 2, R, FF), 1.0, 6.0, ((3, 8),))
    adapter_down = bell_draw(seeds[2], (EXPERTS, 2, R, D), 1.0, 6.0, ((2, 8), (3, 16)))
    file_sizes = ragged(seeds[3], N_EXPERT, 2 * EXPERTS, CAP, 2).astype(jnp.int32)
    file_writer = jax.random.permutation(seeds[4], N_EXPERT).astype(jnp.int32)
    return dict(base_weights=base_weights, adapter_up_factor=adapter_up_factor, adapter_down=adapter_down, file_sizes=file_sizes, file_writer=file_writer)


scaling = 0.125


def merge_one(trio):
    base_tensor, up_tensor, down_tensor = trio
    merge_update = jnp.dot(up_tensor.T, down_tensor, preferred_element_type=jnp.float32)
    return (base_tensor.astype(jnp.float32) + scaling * merge_update).astype(jnp.bfloat16)


def slot_lookup_table(file_sizes, file_writer, writers_count):
    writers = jnp.arange(writers_count, dtype=jnp.int32)
    matches = file_writer[None, :] == writers[:, None]
    starts = (jnp.cumsum(file_sizes) - file_sizes).astype(jnp.int32)
    slot_count = jnp.sum(jnp.where(matches, file_sizes[None, :], 0), axis=1).astype(jnp.int32)
    slot_first = jnp.sum(jnp.where(matches, starts[None, :], 0), axis=1).astype(jnp.int32)
    positions = jnp.arange(CAP, dtype=jnp.int32)
    slot_live = positions[None, :] < slot_count[:, None]
    slot_source = jnp.where(slot_live, slot_first[:, None] + positions[None, :], 0).astype(jnp.int32)
    return slot_source, slot_live


def reference(base_weights, adapter_up_factor, adapter_down, file_sizes, file_writer):
    tensors = 2 * EXPERTS
    flat_base = base_weights.reshape(tensors, FF, D)
    flattened_up = adapter_up_factor.reshape(tensors, R, FF)
    flattened_down = adapter_down.reshape(tensors, R, D)
    merged = lax.map(merge_one, (flat_base, flattened_up, flattened_down))
    slot_source, slot_live = slot_lookup_table(file_sizes, file_writer, N_EXPERT)
    stored = jnp.where(slot_live[:, :, None, None], merged[slot_source], jnp.zeros((), jnp.bfloat16))
    return stored.reshape(N_EXPERT * CAP, FF, D)
```

```python
import jax
import jax.numpy as jnp
from jax import lax
from jax.experimental import pallas as pl
from jax.experimental.pallas import tpu as pltpu
from jax.sharding import PartitionSpec as P

CAP = 8
STEP = 8
scaling = 0.125
VMEM = 40 * 1024 * 1024


def slot_tables(file_sizes, file_writer, tensors):
    writers = jnp.arange(file_writer.shape[0], dtype=jnp.int32)
    starts = jnp.cumsum(file_sizes) - file_sizes
    number = jnp.arange(tensors, dtype=jnp.int32)[:, None]
    inside = (number >= starts[None, :]) & (number < (starts + file_sizes)[None, :])
    place = jnp.sum(jnp.where(inside, file_writer[None, :] * CAP + number - starts[None, :], 0), axis=1)
    size_of = jnp.sum(jnp.where(file_writer[None, :] == writers[:, None], file_sizes[None, :], 0), axis=1)
    return place.astype(jnp.int32), size_of.astype(jnp.int32)


def merge_kernel(place_ref, base_ref, up_ref, down_ref, out_ref, held, sems):
    step = pl.program_id(0)
    steps = pl.num_programs(0)
    slot = lax.rem(step, 2)

    def copy(slot, at, i):
        return pltpu.make_async_copy(held.at[slot, i], out_ref.at[place_ref[at * STEP + i]], sems.at[slot, i])

    @pl.when(step >= 2)
    def _():
        for i in range(STEP):
            copy(slot, step - 2, i).wait()

    for i in range(STEP):
        delta = lax.dot_general(
            up_ref[i], down_ref[i], (((0,), (0,)), ((), ())), preferred_element_type=jnp.float32
        )
        held[slot, i] = (base_ref[i].astype(jnp.float32) + scaling * delta).astype(jnp.bfloat16)
        copy(slot, step, i).start()

    @pl.when(step == steps - 1)
    def _():
        for i in range(STEP):
            copy(1 - slot, step - 1, i).wait()
        for i in range(STEP):
            copy(slot, step, i).wait()


def merge(place, base, up, down, slots):
    tensors, rows, cols = base.shape
    rank = up.shape[1]
    return pl.pallas_call(
        merge_kernel,
        out_shape=jax.ShapeDtypeStruct((slots, rows, cols), jnp.bfloat16),
        grid_spec=pltpu.PrefetchScalarGridSpec(
            num_scalar_prefetch=1,
            grid=(tensors // STEP,),
            in_specs=[
                pl.BlockSpec((STEP, rows, cols), lambda s, p: (s, 0, 0)),
                pl.BlockSpec((STEP, rank, rows), lambda s, p: (s, 0, 0)),
                pl.BlockSpec((STEP, rank, cols), lambda s, p: (s, 0, 0)),
            ],
            out_specs=pl.BlockSpec(memory_space=pl.ANY),
            scratch_shapes=[
                pltpu.VMEM((2, STEP, rows, cols), jnp.bfloat16),
                pltpu.SemaphoreType.DMA((2, STEP)),
            ],
        ),
        compiler_params=pltpu.CompilerParams(vmem_limit_bytes=VMEM),
        name="merge",
    )(place, base, up, down)


def unpack_kernel(count_ref, arrived_ref, out_ref):
    slot = pl.program_id(0)
    sources, _, _, cols = arrived_ref.shape

    @pl.when(slot < count_ref[0])
    def _():
        for e in range(sources):
            out_ref[0, :, e * cols : (e + 1) * cols] = arrived_ref[e, 0]

    @pl.when(slot >= count_ref[0])
    def _():
        out_ref[...] = jnp.zeros_like(out_ref)


def unpack(count, arrived):
    sources, slots, rows, cols = arrived.shape
    return pl.pallas_call(
        unpack_kernel,
        out_shape=jax.ShapeDtypeStruct((slots, rows, sources * cols), jnp.bfloat16),
        grid_spec=pltpu.PrefetchScalarGridSpec(
            num_scalar_prefetch=1,
            grid=(slots,),
            in_specs=[pl.BlockSpec((sources, 1, rows, cols), lambda s, n: (0, s, 0, 0))],
            out_specs=pl.BlockSpec((1, rows, sources * cols), lambda s, n: (s, 0, 0)),
        ),
        compiler_params=pltpu.CompilerParams(vmem_limit_bytes=VMEM),
        name="unpack",
    )(count, arrived)


def body(base_weights, adapter_up_factor, adapter_down, file_sizes, file_writer):
    writers = lax.axis_size("expert")
    tensors = base_weights.shape[0] * base_weights.shape[1]
    base = base_weights.reshape(tensors, *base_weights.shape[2:])
    up = adapter_up_factor.reshape(tensors, *adapter_up_factor.shape[2:])
    down_here = adapter_down.reshape(tensors, *adapter_down.shape[2:])
    place, size_of = slot_tables(file_sizes, file_writer, tensors)
    down = lax.all_gather(down_here, "row", axis=1, tiled=True)
    outgoing = merge(place, base, up, down, writers * CAP)
    outgoing = outgoing.reshape(writers, CAP, *outgoing.shape[1:])
    arrived = lax.all_to_all(outgoing, "expert", split_axis=0, concat_axis=0)
    count = lax.dynamic_slice(size_of, (lax.axis_index("expert"),), (1,))
    return unpack(count, arrived)


def solution(mesh):
    in_specs = (
        P(None, None, "row", "expert"),
        P(None, None, None, "row"),
        P(None, None, "row", "expert"),
        P(),
        P(),
    )
    out_specs = P("expert", "row", None)
    return jax.shard_map(body, mesh=mesh, in_specs=in_specs, out_specs=out_specs, check_vma=False)
```

```python
import jax
import jax.numpy as jnp
from jax import lax
from jax.experimental import pallas as pl
from jax.experimental.pallas import tpu as pltpu
from jax.sharding import PartitionSpec as P

CAP = 8
SIDE = 4
STEP = 8
CHUNKS = 1
CAPACITIES = (18, 20, 22, 24, 26, 28, 32)
ORDER = (1, 3, 2)
scaling = 0.125
VMEM = 24 * 1024 * 1024


def shift(dz, dx):
    return [
        (z * SIDE + x, (z + dz) % SIDE * SIDE + (x + dx) % SIDE)
        for z in range(SIDE)
        for x in range(SIDE)
    ]


def send(block, half, first, k):
    along_z = (half == 0) == first
    return lax.ppermute(block, "expert", shift(k, 0) if along_z else shift(0, k))


def route(file_sizes, file_writer, tensors, z, x):
    files = file_sizes.shape[0]
    ids = jnp.arange(files, dtype=jnp.int32)
    starts = jnp.sum(jnp.where(ids[None, :] < ids[:, None], file_sizes[None, :], 0), axis=1)
    owns = file_writer[None, :] == ids[:, None]
    size_of = jnp.sum(jnp.where(owns, file_sizes[None, :], 0), axis=1)
    wz, wx = ids // SIDE, ids % SIDE
    in_row = (wz[:, None] == wz[None, :]) & (wx[None, :] < wx[:, None])
    in_col = (wx[:, None] == wx[None, :]) & (wz[None, :] < wz[:, None])
    first_row = jnp.sum(jnp.where(in_row, size_of[None, :], 0), axis=1)
    first_col = jnp.sum(jnp.where(in_col, size_of[None, :], 0), axis=1)
    most = jnp.maximum(jnp.max(first_row + size_of), jnp.max(first_col + size_of))

    number = jnp.arange(tensors, dtype=jnp.int32)[:, None]
    inside = (number >= starts[None, :]) & (number < (starts + file_sizes)[None, :])
    slot = number - starts[None, :]

    def of_file(values):
        return jnp.sum(jnp.where(owns, values[:, None], 0), axis=0)

    def of_tensor(values):
        return jnp.sum(jnp.where(inside, values, 0), axis=1)

    to_z, to_x = file_writer // SIDE, file_writer % SIDE
    meta = jnp.stack([
        of_tensor(((to_z - z) % SIDE)[None, :]),
        of_tensor(of_file(first_row)[None, :] + slot),
        of_tensor(((to_x - x) % SIDE)[None, :]),
        of_tensor(of_file(first_col)[None, :] + slot),
    ]).astype(jnp.int32)
    rel = jnp.arange(SIDE, dtype=jnp.int32)
    along_x = (z * SIDE + (x + rel) % SIDE)[:, None] == ids[None, :]
    along_z = ((z + rel) % SIDE * SIDE + x)[:, None] == ids[None, :]
    begin = jnp.stack([
        jnp.sum(jnp.where(along_x, first_row[None, :], 0), axis=1),
        jnp.sum(jnp.where(along_z, first_col[None, :], 0), axis=1),
    ]).astype(jnp.int32)
    count = jnp.sum(jnp.where(ids == z * SIDE + x, size_of, 0)).astype(jnp.int32)
    return meta, begin, count, most


def merge_kernel(rows_at, meta_ref, base_a_ref, base_b_ref, up_ref, down_ref, *rest):
    outs, held, sems = rest[: 2 * SIDE], rest[-2], rest[-1]
    step = pl.program_id(0)
    steps = pl.num_programs(0)
    slot = lax.rem(step, 2)
    height = held.shape[3]

    def each(slot, step, i, act):
        for half in range(2):
            to = meta_ref[2 * half, step * STEP + i]
            place = meta_ref[2 * half + 1, step * STEP + i]
            for k in range(SIDE):

                @pl.when(to == k)
                def _():
                    act(pltpu.make_async_copy(
                        held.at[slot, i, half], outs[half * SIDE + k].at[place], sems.at[slot, i, half]
                    ))

    @pl.when(step >= 2)
    def _():
        for i in range(STEP):
            each(slot, step - 2, i, lambda c: c.wait())

    for i in range(STEP):
        for half, base_ref in enumerate((base_a_ref, base_b_ref)):
            delta = lax.dot_general(
                up_ref[i][:, rows_at[half] : rows_at[half] + height],
                down_ref[i],
                (((0,), (0,)), ((), ())),
                preferred_element_type=jnp.float32,
            )
            held[slot, i, half] = (base_ref[i].astype(jnp.float32) + scaling * delta).astype(jnp.bfloat16)
        each(slot, step, i, lambda c: c.start())

    @pl.when(step == steps - 1)
    def _():
        for i in range(STEP):
            each(1 - slot, step - 1, i, lambda c: c.wait())
        for i in range(STEP):
            each(slot, step, i, lambda c: c.wait())


def merge(meta, base, up, down, chunk, capacity):
    tensors, rows, cols = base.shape
    rank = up.shape[1]
    height = rows // (2 * CHUNKS)
    rows_at = (chunk * height, (CHUNKS + chunk) * height)

    def kernel(*refs):
        merge_kernel(rows_at, *refs)

    return pl.pallas_call(
        kernel,
        out_shape=[jax.ShapeDtypeStruct((capacity, height, cols), jnp.bfloat16)] * (2 * SIDE),
        grid_spec=pltpu.PrefetchScalarGridSpec(
            num_scalar_prefetch=1,
            grid=(tensors // STEP,),
            in_specs=[
                pl.BlockSpec((STEP, height, cols), lambda s, p: (s, chunk, 0)),
                pl.BlockSpec((STEP, height, cols), lambda s, p: (s, CHUNKS + chunk, 0)),
                pl.BlockSpec((STEP, rank, rows), lambda s, p: (s, 0, 0)),
                pl.BlockSpec((STEP, rank, cols), lambda s, p: (s, 0, 0)),
            ],
            out_specs=[pl.BlockSpec(memory_space=pl.ANY)] * (2 * SIDE),
            scratch_shapes=[
                pltpu.VMEM((2, STEP, 2, height, cols), jnp.bfloat16),
                pltpu.SemaphoreType.DMA((2, STEP, 2)),
            ],
        ),
        compiler_params=pltpu.CompilerParams(vmem_limit_bytes=VMEM),
        cost_estimate=pl.CostEstimate(
            flops=2 * tensors * rank * cols * 2 * height,
            bytes_accessed=2 * tensors * cols * (4 * height + rank + rows // 4),
            transcendentals=0,
        ),
        name="merge",
    )(meta, base, base, up, down)


def regroup_kernel(begin_ref, *refs):
    lists, outs, sems = refs[: 2 * SIDE], refs[2 * SIDE : -1], refs[-1]
    copies = []
    for half in range(2):
        for r in ORDER:
            for k in range(SIDE):
                copies.append(pltpu.make_async_copy(
                    lists[half * SIDE + k].at[pl.ds(begin_ref[half, r], CAP)],
                    outs[half * (SIDE - 1) + r - 1].at[k],
                    sems.at[half, r - 1, k],
                ))
    for copy in copies:
        copy.start()
    for copy in copies:
        copy.wait()


def regroup(begin, lists):
    _, height, cols = lists[0].shape
    out = jax.ShapeDtypeStruct((SIDE, CAP, height, cols), jnp.bfloat16)
    number = 2 * (SIDE - 1)
    return pl.pallas_call(
        regroup_kernel,
        out_shape=[out] * number,
        grid_spec=pltpu.PrefetchScalarGridSpec(
            num_scalar_prefetch=1,
            grid=(1,),
            in_specs=[pl.BlockSpec(memory_space=pl.ANY)] * (2 * SIDE),
            out_specs=[pl.BlockSpec(memory_space=pl.ANY)] * number,
            scratch_shapes=[pltpu.SemaphoreType.DMA((2, SIDE - 1, SIDE))],
        ),
        compiler_params=pltpu.CompilerParams(vmem_limit_bytes=VMEM),
        cost_estimate=pl.CostEstimate(
            flops=0, bytes_accessed=2 * number * SIDE * CAP * height * cols * 2, transcendentals=0
        ),
        name="regroup",
    )(begin, *lists)


def unpack_kernel(meta_ref, *refs):
    out_ref = refs[-1]
    half, slot = pl.program_id(0), pl.program_id(1)
    z, x = meta_ref[3], meta_ref[4]
    cols = out_ref.shape[2] // (SIDE * SIDE)
    per = 2 * SIDE - 1

    for which in range(2):
        own, others = refs[which * per : which * per + SIDE], refs[which * per + SIDE : (which + 1) * per]

        @pl.when((slot < meta_ref[0]) & (half == which))
        def _():
            for k in range(SIDE):
                for r in range(SIDE):
                    back_z, back_x = (k, r) if which == 0 else (r, k)
                    source = lax.rem(z + SIDE - back_z, SIDE) * SIDE + lax.rem(x + SIDE - back_x, SIDE)
                    at = pl.ds(pl.multiple_of(source * cols, cols), cols)
                    out_ref[0, :, at] = own[k][0] if r == 0 else others[r - 1][k, 0]

    @pl.when(slot >= meta_ref[0])
    def _():
        out_ref[...] = jnp.zeros_like(out_ref)


def unpack(meta, begins, own, others, chunk, before):
    _, height, cols = own[0].shape

    def at(h, s, m, half):
        return jnp.minimum(jnp.where(h == half, s, jnp.where(h > half, CAP - 1, 0)), m[0] - 1)

    scalars = jnp.concatenate([meta, begins])
    specs, operands = [], []
    for half in range(2):
        for k in range(SIDE):
            specs.append(pl.BlockSpec(
                (1, height, cols),
                lambda h, s, m, half=half: (m[5 + half] + at(h, s, m, half), 0, 0),
            ))
            operands.append(own[half * SIDE + k])
        for r in range(1, SIDE):
            specs.append(pl.BlockSpec(
                (SIDE, 1, height, cols),
                lambda h, s, m, half=half: (
                    0, m[1 + half] + at(h, s, m, half), 0, 0),
            ))
            operands.append(others[half * (SIDE - 1) + r - 1])
    aliases = {}
    if before is not None:
        specs.append(pl.BlockSpec(memory_space=pl.ANY))
        operands.append(before)
        aliases = {1 + len(operands) - 1: 0}
    return pl.pallas_call(
        unpack_kernel,
        out_shape=jax.ShapeDtypeStruct((CAP, 2 * CHUNKS * height, SIDE * SIDE * cols), jnp.bfloat16),
        grid_spec=pltpu.PrefetchScalarGridSpec(
            num_scalar_prefetch=1,
            grid=(2, CAP),
            in_specs=specs,
            out_specs=pl.BlockSpec((1, height, SIDE * SIDE * cols), lambda h, s, m: (s, h * CHUNKS + chunk, 0)),
        ),
        input_output_aliases=aliases,
        compiler_params=pltpu.CompilerParams(vmem_limit_bytes=VMEM),
        cost_estimate=pl.CostEstimate(
            flops=0, bytes_accessed=2 * 2 * CAP * height * SIDE * SIDE * cols * 2, transcendentals=0
        ),
        name="unpack",
    )(scalars, *operands)


def deliver(capacity, base, up, down, meta, begin, count, z, x):
    start = jnp.minimum(begin, capacity - CAP)
    skip = begin[:, 0] - start[:, 0]
    tail = jnp.stack([count, skip[0], skip[1], z, x])
    out = None
    for chunk in range(CHUNKS):
        sends = merge(meta, base, up, down, chunk, capacity)
        lists = [None] * (2 * SIDE)
        for half in range(2):
            lists[half * SIDE] = sends[half * SIDE]
        for k in ORDER:
            for half in range(2):
                lists[half * SIDE + k] = send(sends[half * SIDE + k], half, True, k)
        groups = regroup(start, lists)
        others = [None] * (2 * (SIDE - 1))
        for r in ORDER:
            for half in range(2):
                others[half * (SIDE - 1) + r - 1] = send(groups[half * (SIDE - 1) + r - 1], half, False, r)
        out = unpack(tail, begin[:, 0], lists, others, chunk, out)
    return out


def body(base_weights, adapter_up_factor, adapter_down, file_sizes, file_writer):
    tensors = base_weights.shape[0] * base_weights.shape[1]
    base = base_weights.reshape(tensors, *base_weights.shape[2:])
    up = adapter_up_factor.reshape(tensors, *adapter_up_factor.shape[2:])
    down_here = adapter_down.reshape(tensors, *adapter_down.shape[2:])
    rank = lax.axis_index("expert")
    z, x = rank // SIDE, rank % SIDE
    meta, begin, count, most = route(file_sizes, file_writer, tensors, z, x)
    down = lax.all_gather(down_here, "row", axis=1, tiled=True)
    which = jnp.sum(most > jnp.array(CAPACITIES[:-1], jnp.int32)).astype(jnp.int32)
    branches = [lambda *a, c=c: deliver(c, *a) for c in CAPACITIES]
    return lax.switch(which, branches, base, up, down, meta, begin, count, z, x)


def solution(mesh):
    in_specs = (
        P(None, None, "row", "expert"),
        P(None, None, None, "row"),
        P(None, None, "row", "expert"),
        P(),
        P(),
    )
    out_specs = P("expert", "row", None)
    return jax.shard_map(body, mesh=mesh, in_specs=in_specs, out_specs=out_specs, check_vma=False)
```

```python
import jax
import jax.numpy as jnp
from jax import lax
from jax.experimental import pallas as pl
from jax.experimental.pallas import tpu as pltpu
from jax.sharding import PartitionSpec as P

CAP = 8
SIDE = 4
STEP = 8
CHUNKS = 2
CAPACITIES = (20, 22, 24, 26, 32)
LONGEST = CAPACITIES[-1]
ORDER = (1, 3, 2)
scaling = 0.125
VMEM = 56 * 1024 * 1024


def shift(dz, dx):
    return [
        (z * SIDE + x, (z + dz) % SIDE * SIDE + (x + dx) % SIDE)
        for z in range(SIDE)
        for x in range(SIDE)
    ]


def send(block, half, first, k):
    along_z = (half == 0) == first
    return lax.ppermute(block, "expert", shift(k, 0) if along_z else shift(0, k))


def route(file_sizes, file_writer, tensors, z, x):
    files = file_sizes.shape[0]
    ids = jnp.arange(files, dtype=jnp.int32)
    starts = jnp.sum(jnp.where(ids[None, :] < ids[:, None], file_sizes[None, :], 0), axis=1)
    owns = file_writer[None, :] == ids[:, None]
    size_of = jnp.sum(jnp.where(owns, file_sizes[None, :], 0), axis=1)
    wz, wx = ids // SIDE, ids % SIDE
    in_row = (wz[:, None] == wz[None, :]) & (wx[None, :] < wx[:, None])
    in_col = (wx[:, None] == wx[None, :]) & (wz[None, :] < wz[:, None])
    first_row = jnp.sum(jnp.where(in_row, size_of[None, :], 0), axis=1)
    first_col = jnp.sum(jnp.where(in_col, size_of[None, :], 0), axis=1)
    most = jnp.maximum(jnp.max(first_row + size_of), jnp.max(first_col + size_of))

    number = jnp.arange(tensors, dtype=jnp.int32)[:, None]
    inside = (number >= starts[None, :]) & (number < (starts + file_sizes)[None, :])
    slot = number - starts[None, :]

    def of_file(values):
        return jnp.sum(jnp.where(owns, values[:, None], 0), axis=0)

    def of_tensor(values):
        return jnp.sum(jnp.where(inside, values, 0), axis=1)

    to_z, to_x = file_writer // SIDE, file_writer % SIDE
    lists, lengths = [], []
    for to, first in (((to_z - z) % SIDE, first_row), ((to_x - x) % SIDE, first_col)):
        to_of, place_of = of_tensor(to[None, :]), of_tensor(of_file(first)[None, :] + slot)
        for k in range(SIDE):
            mine = to_of == k
            here = mine[None, :] & (place_of[None, :] == jnp.arange(LONGEST, dtype=jnp.int32)[:, None])
            lists.append(jnp.sum(jnp.where(here, number[None, :, 0], 0), axis=1))
            lengths.append(jnp.sum(mine))
    meta = jnp.concatenate([*lists, jnp.stack(lengths)]).astype(jnp.int32)
    rel = jnp.arange(SIDE, dtype=jnp.int32)
    along_x = (z * SIDE + (x + rel) % SIDE)[:, None] == ids[None, :]
    along_z = ((z + rel) % SIDE * SIDE + x)[:, None] == ids[None, :]
    begin = jnp.stack([
        jnp.sum(jnp.where(along_x, first_row[None, :], 0), axis=1),
        jnp.sum(jnp.where(along_z, first_col[None, :], 0), axis=1),
    ]).astype(jnp.int32)
    count = jnp.sum(jnp.where(ids == z * SIDE + x, size_of, 0)).astype(jnp.int32)
    return meta, begin, count, most


def merge_kernel(capacity, meta_ref, base_ref, up_ref, down_ref, *rest):
    outs, held, sem = rest[: 2 * SIDE], rest[-2], rest[-1]
    step = pl.program_id(0)
    height = outs[0].shape[1]
    for i in range(STEP):
        delta = lax.dot_general(
            up_ref[i], down_ref[i], (((0,), (0,)), ((), ())), preferred_element_type=jnp.float32
        )
        merged = base_ref[i].astype(jnp.float32) + scaling * delta
        held[step * STEP + i] = merged.astype(jnp.bfloat16)

    @pl.when(step == pl.num_programs(0) - 1)
    def _():
        def each(which, act):
            half, k = divmod(which, SIDE)

            @pl.loop(0, meta_ref[2 * SIDE * LONGEST + which])
            def _(m):
                tensor = meta_ref[which * LONGEST + m]
                act(pltpu.make_async_copy(
                    held.at[tensor, pl.ds(half * height, height)], outs[which].at[m], sem.at[which]
                ))

        for k in ORDER + (0,):
            for half in range(2):
                each(half * SIDE + k, lambda c: c.start())
        for which in range(2 * SIDE):
            each(which, lambda c: c.wait())


def merge(meta, base, up, down, chunk, capacity):
    tensors, rows, _ = base.shape
    rank, cols = down.shape[1:]
    height = rows // 2

    def kernel(*refs):
        merge_kernel(capacity, *refs)

    return pl.pallas_call(
        kernel,
        out_shape=[jax.ShapeDtypeStruct((capacity, height, cols), jnp.bfloat16)] * (2 * SIDE),
        grid_spec=pltpu.PrefetchScalarGridSpec(
            num_scalar_prefetch=1,
            grid=(tensors // STEP,),
            in_specs=[
                pl.BlockSpec((STEP, rows, cols), lambda s, p: (s, 0, chunk)),
                pl.BlockSpec((STEP, rank, rows), lambda s, p: (s, 0, 0)),
                pl.BlockSpec((STEP, rank, cols), lambda s, p: (s, 0, 0)),
            ],
            out_specs=[pl.BlockSpec(memory_space=pl.ANY)] * (2 * SIDE),
            scratch_shapes=[
                pltpu.VMEM((tensors, rows, cols), jnp.bfloat16),
                pltpu.SemaphoreType.DMA((2 * SIDE,)),
            ],
        ),
        compiler_params=pltpu.CompilerParams(vmem_limit_bytes=VMEM),
        cost_estimate=pl.CostEstimate(
            flops=2 * tensors * rank * cols * rows,
            bytes_accessed=2 * tensors * (2 * cols * rows + rank * cols + rank * rows),
            transcendentals=0,
        ),
        name="merge",
    )(meta, base, up, down)


def regroup_kernel(begin_ref, *refs):
    lists, outs, sems = refs[: 2 * SIDE], refs[2 * SIDE : -1], refs[-1]
    copies = []
    for half in range(2):
        for r in ORDER:
            for k in range(SIDE):
                copies.append(pltpu.make_async_copy(
                    lists[half * SIDE + k].at[pl.ds(begin_ref[half, r], CAP)],
                    outs[half * (SIDE - 1) + r - 1].at[k],
                    sems.at[half, r - 1, k],
                ))
    for copy in copies:
        copy.start()
    for copy in copies:
        copy.wait()


def regroup(begin, lists):
    _, height, cols = lists[0].shape
    out = jax.ShapeDtypeStruct((SIDE, CAP, height, cols), jnp.bfloat16)
    number = 2 * (SIDE - 1)
    return pl.pallas_call(
        regroup_kernel,
        out_shape=[out] * number,
        grid_spec=pltpu.PrefetchScalarGridSpec(
            num_scalar_prefetch=1,
            grid=(1,),
            in_specs=[pl.BlockSpec(memory_space=pl.ANY)] * (2 * SIDE),
            out_specs=[pl.BlockSpec(memory_space=pl.ANY)] * number,
            scratch_shapes=[pltpu.SemaphoreType.DMA((2, SIDE - 1, SIDE))],
        ),
        compiler_params=pltpu.CompilerParams(vmem_limit_bytes=VMEM),
        cost_estimate=pl.CostEstimate(
            flops=0, bytes_accessed=2 * number * SIDE * CAP * height * cols * 2, transcendentals=0
        ),
        name="regroup",
    )(begin, *lists)


def clear_kernel(count_ref, out_ref, zeros, sem):
    zeros[...] = jnp.zeros_like(zeros)
    height = zeros.shape[0]
    parts = out_ref.shape[1] // height

    def each(act):
        @pl.loop(count_ref[0], CAP)
        def _(slot):
            for part in range(parts):
                act(pltpu.make_async_copy(zeros, out_ref.at[slot, pl.ds(part * height, height)], sem))

    each(lambda c: c.start())
    each(lambda c: c.wait())


def clear(count, rows, cols):
    return pl.pallas_call(
        clear_kernel,
        out_shape=jax.ShapeDtypeStruct((CAP, rows, cols), jnp.bfloat16),
        grid_spec=pltpu.PrefetchScalarGridSpec(
            num_scalar_prefetch=1,
            grid=(1,),
            in_specs=[],
            out_specs=pl.BlockSpec(memory_space=pl.ANY),
            scratch_shapes=[pltpu.VMEM((rows // 2, cols), jnp.bfloat16), pltpu.SemaphoreType.DMA],
        ),
        compiler_params=pltpu.CompilerParams(vmem_limit_bytes=VMEM),
        cost_estimate=pl.CostEstimate(flops=0, bytes_accessed=CAP * rows * cols * 2, transcendentals=0),
        name="clear",
    )(count)


def unpack_kernel(chunk, shifts, meta_ref, *refs):
    blocks, out_ref, sems = refs[: 2 * SIDE], refs[-2], refs[-1]
    z, x = meta_ref[3], meta_ref[4]
    width = out_ref.shape[2] // (SIDE * SIDE)
    own = shifts == (0,)
    for bit in (8, 4, 2, 1):

        @pl.when(lax.rem(meta_ref[0], 2 * bit) >= bit)
        def _():
            before = meta_ref[0] - lax.rem(meta_ref[0], 2 * bit)
            copies = []
            for half in range(2):
                first = meta_ref[5 + half] if own else meta_ref[1 + half]
                for i, r in enumerate(shifts):
                    for k in range(SIDE):
                        if own:
                            block = blocks[half * SIDE + k]
                        else:
                            block = blocks[half * len(shifts) + i].at[k]
                        _, height, cols = block.shape
                        back_z, back_x = (k, r) if half == 0 else (r, k)
                        source = lax.rem(z + SIDE - back_z, SIDE) * SIDE + lax.rem(x + SIDE - back_x, SIDE)
                        at = pl.multiple_of(source * width + chunk * cols, cols)
                        copies.append(pltpu.make_async_copy(
                            block.at[pl.ds(first + before, bit)],
                            out_ref.at[pl.ds(before, bit), pl.ds(half * height, height), pl.ds(at, cols)],
                            sems.at[half, i, k],
                        ))
            for copy in copies:
                copy.start()
            for copy in copies:
                copy.wait()


def unpack(meta, blocks, chunk, shifts, before):
    height, cols = blocks[0].shape[-2:]

    def kernel(meta_ref, *refs):
        number = len(blocks)
        unpack_kernel(chunk, shifts, meta_ref, *refs[:number], refs[-2], refs[-1])

    return pl.pallas_call(
        kernel,
        out_shape=jax.ShapeDtypeStruct(before.shape, before.dtype),
        grid_spec=pltpu.PrefetchScalarGridSpec(
            num_scalar_prefetch=1,
            grid=(1,),
            in_specs=[pl.BlockSpec(memory_space=pl.ANY)] * (len(blocks) + 1),
            out_specs=pl.BlockSpec(memory_space=pl.ANY),
            scratch_shapes=[pltpu.SemaphoreType.DMA((2, len(shifts), SIDE))],
        ),
        input_output_aliases={1 + len(blocks): 0},
        compiler_params=pltpu.CompilerParams(vmem_limit_bytes=VMEM),
        cost_estimate=pl.CostEstimate(
            flops=0, bytes_accessed=2 * 2 * len(shifts) * SIDE * CAP * height * cols * 2, transcendentals=0
        ),
        name="unpack",
    )(meta, *blocks, before)


def deliver(capacity, base, up, down_first, down_here, meta, begin, count, z, x, out):
    start = jnp.minimum(begin, capacity - CAP)
    skip = begin[:, 0] - start[:, 0]
    tail = jnp.concatenate([jnp.stack([count, skip[0], skip[1], z, x]), begin[:, 0]])
    gathered = [down_first]
    for chunk in range(1, CHUNKS):
        gathered.append(gather(down_here, chunk))
    pending = []
    for chunk in range(CHUNKS):
        sends = merge(meta, base, up, gathered[chunk], chunk, capacity)
        lists = [None] * (2 * SIDE)
        for half in range(2):
            lists[half * SIDE] = sends[half * SIDE]
        for k in ORDER:
            for half in range(2):
                lists[half * SIDE + k] = send(sends[half * SIDE + k], half, True, k)
        pending.append(lists)
    for chunk, lists in enumerate(pending):
        groups = regroup(start, lists)
        others = [None] * (2 * (SIDE - 1))
        for r in ORDER:
            for half in range(2):
                others[half * (SIDE - 1) + r - 1] = send(groups[half * (SIDE - 1) + r - 1], half, False, r)
        out = unpack(tail, lists, chunk, (0,), out)
        out = unpack(tail, others, chunk, (1, 2, 3), out)
    return out


def gather(down_here, chunk):
    cols = down_here.shape[2] // CHUNKS
    return lax.all_gather(down_here[:, :, chunk * cols : (chunk + 1) * cols], "row", axis=1, tiled=True)


def body(base_weights, adapter_up_factor, adapter_down, file_sizes, file_writer):
    tensors = base_weights.shape[0] * base_weights.shape[1]
    base = base_weights.reshape(tensors, *base_weights.shape[2:])
    up = adapter_up_factor.reshape(tensors, *adapter_up_factor.shape[2:])
    down_here = adapter_down.reshape(tensors, *adapter_down.shape[2:])
    rank = lax.axis_index("expert")
    z, x = rank // SIDE, rank % SIDE
    meta, begin, count, most = route(file_sizes, file_writer, tensors, z, x)
    down = gather(down_here, 0)
    out = clear(count[None], base.shape[1], base.shape[2] * SIDE * SIDE)
    which = jnp.sum(most > jnp.array(CAPACITIES[:-1], jnp.int32)).astype(jnp.int32)
    branches = [lambda *a, c=c: deliver(c, *a) for c in CAPACITIES]
    return lax.switch(which, branches, base, up, down, down_here, meta, begin, count, z, x, out)


def solution(mesh):
    in_specs = (
        P(None, None, "row", "expert"),
        P(None, None, None, "row"),
        P(None, None, "row", "expert"),
        P(),
        P(),
    )
    out_specs = P("expert", "row", None)
    return jax.shard_map(body, mesh=mesh, in_specs=in_specs, out_specs=out_specs, check_vma=False)
```

```python
import jax
import jax.numpy as jnp
from jax import lax
from jax.experimental import pallas as pl
from jax.experimental.pallas import tpu as pltpu
from jax.sharding import PartitionSpec as P

CAP = 8
SIDE = 4
STEP = 8
CHUNKS = 2
CAPACITIES = (20, 22, 24, 26, 32)
LONGEST = CAPACITIES[-1]
ORDER = (1, 3, 2)
scaling = 0.125
VMEM = 56 * 1024 * 1024


def shift(dz, dx):
    return [
        (z * SIDE + x, (z + dz) % SIDE * SIDE + (x + dx) % SIDE)
        for z in range(SIDE)
        for x in range(SIDE)
    ]


def send(block, half, first, k):
    along_z = (half == 0) == first
    return lax.ppermute(block, "expert", shift(k, 0) if along_z else shift(0, k))


def route(file_sizes, file_writer, tensors, z, x):
    files = file_sizes.shape[0]
    ids = jnp.arange(files, dtype=jnp.int32)
    starts = jnp.sum(jnp.where(ids[None, :] < ids[:, None], file_sizes[None, :], 0), axis=1)
    owns = file_writer[None, :] == ids[:, None]
    size_of = jnp.sum(jnp.where(owns, file_sizes[None, :], 0), axis=1)
    wz, wx = ids // SIDE, ids % SIDE
    in_row = (wz[:, None] == wz[None, :]) & (wx[None, :] < wx[:, None])
    in_col = (wx[:, None] == wx[None, :]) & (wz[None, :] < wz[:, None])
    first_row = jnp.sum(jnp.where(in_row, size_of[None, :], 0), axis=1)
    first_col = jnp.sum(jnp.where(in_col, size_of[None, :], 0), axis=1)
    most = jnp.maximum(jnp.max(first_row + size_of), jnp.max(first_col + size_of))

    number = jnp.arange(tensors, dtype=jnp.int32)[:, None]
    inside = (number >= starts[None, :]) & (number < (starts + file_sizes)[None, :])
    slot = number - starts[None, :]

    def of_file(values):
        return jnp.sum(jnp.where(owns, values[:, None], 0), axis=0)

    def of_tensor(values):
        return jnp.sum(jnp.where(inside, values, 0), axis=1)

    to_z, to_x = file_writer // SIDE, file_writer % SIDE
    lists, lengths = [], []
    for to, first in (((to_z - z) % SIDE, first_row), ((to_x - x) % SIDE, first_col)):
        to_of, place_of = of_tensor(to[None, :]), of_tensor(of_file(first)[None, :] + slot)
        for k in range(SIDE):
            mine = to_of == k
            here = mine[None, :] & (place_of[None, :] == jnp.arange(LONGEST, dtype=jnp.int32)[:, None])
            lists.append(jnp.sum(jnp.where(here, number[None, :, 0], 0), axis=1))
            lengths.append(jnp.sum(mine))
    meta = jnp.concatenate([*lists, jnp.stack(lengths)]).astype(jnp.int32)
    rel = jnp.arange(SIDE, dtype=jnp.int32)
    along_x = (z * SIDE + (x + rel) % SIDE)[:, None] == ids[None, :]
    along_z = ((z + rel) % SIDE * SIDE + x)[:, None] == ids[None, :]
    begin = jnp.stack([
        jnp.sum(jnp.where(along_x, first_row[None, :], 0), axis=1),
        jnp.sum(jnp.where(along_z, first_col[None, :], 0), axis=1),
    ]).astype(jnp.int32)
    count = jnp.sum(jnp.where(ids == z * SIDE + x, size_of, 0)).astype(jnp.int32)
    return meta, begin, count, most


def merge_kernel(capacity, meta_ref, base_ref, up_ref, down_ref, *rest):
    outs, held, sem = rest[: 2 * SIDE], rest[-2], rest[-1]
    step = pl.program_id(0)
    height = outs[0].shape[1]
    for i in range(STEP):
        delta = lax.dot_general(
            up_ref[i], down_ref[i], (((0,), (0,)), ((), ())), preferred_element_type=jnp.float32
        )
        merged = base_ref[i].astype(jnp.float32) + scaling * delta
        held[step * STEP + i] = merged.astype(jnp.bfloat16)

    @pl.when(step == pl.num_programs(0) - 1)
    def _():
        def each(which, act):
            half, k = divmod(which, SIDE)

            @pl.loop(0, meta_ref[2 * SIDE * LONGEST + which])
            def _(m):
                tensor = meta_ref[which * LONGEST + m]
                act(pltpu.make_async_copy(
                    held.at[tensor, pl.ds(half * height, height)], outs[which].at[m], sem.at[which]
                ))

        for k in ORDER + (0,):
            for half in range(2):
                each(half * SIDE + k, lambda c: c.start())
        for which in range(2 * SIDE):
            each(which, lambda c: c.wait())


def merge(meta, base, up, down, chunk, capacity):
    tensors, rows, _ = base.shape
    rank, cols = down.shape[1:]
    height = rows // 2

    def kernel(*refs):
        merge_kernel(capacity, *refs)

    return pl.pallas_call(
        kernel,
        out_shape=[jax.ShapeDtypeStruct((capacity, height, cols), jnp.bfloat16)] * (2 * SIDE),
        grid_spec=pltpu.PrefetchScalarGridSpec(
            num_scalar_prefetch=1,
            grid=(tensors // STEP,),
            in_specs=[
                pl.BlockSpec((STEP, rows, cols), lambda s, p: (s, 0, chunk)),
                pl.BlockSpec((STEP, rank, rows), lambda s, p: (s, 0, 0)),
                pl.BlockSpec((STEP, rank, cols), lambda s, p: (s, 0, 0)),
            ],
            out_specs=[pl.BlockSpec(memory_space=pl.ANY)] * (2 * SIDE),
            scratch_shapes=[
                pltpu.VMEM((tensors, rows, cols), jnp.bfloat16),
                pltpu.SemaphoreType.DMA((2 * SIDE,)),
            ],
        ),
        compiler_params=pltpu.CompilerParams(vmem_limit_bytes=VMEM),
        cost_estimate=pl.CostEstimate(
            flops=2 * tensors * rank * cols * rows,
            bytes_accessed=2 * tensors * (2 * cols * rows + rank * cols + rank * rows),
            transcendentals=0,
        ),
        name="merge",
    )(meta, base, up, down)


def regroup_kernel(begin_ref, *refs):
    lists, outs, held, got, put = refs[: 2 * SIDE], refs[2 * SIDE : -3], refs[-3], refs[-2], refs[-1]
    ins, leaves = [], []
    for r in ORDER:
        for half in range(2):
            for k in range(SIDE):
                ins.append(pltpu.make_async_copy(
                    lists[half * SIDE + k].at[pl.ds(begin_ref[half, r], CAP)],
                    held.at[half, r - 1, k],
                    got.at[half, r - 1, k],
                ))
            leaves.append(pltpu.make_async_copy(
                held.at[half, r - 1], outs[half * (SIDE - 1) + r - 1], put.at[half, r - 1]
            ))
    for copy in ins:
        copy.start()
    for at, copy in enumerate(leaves):
        for part in ins[at * SIDE : (at + 1) * SIDE]:
            part.wait()
        copy.start()
    for copy in leaves:
        copy.wait()


def regroup(begin, lists):
    _, height, cols = lists[0].shape
    out = jax.ShapeDtypeStruct((SIDE, CAP, height, cols), jnp.bfloat16)
    number = 2 * (SIDE - 1)
    return pl.pallas_call(
        regroup_kernel,
        out_shape=[out] * number,
        grid_spec=pltpu.PrefetchScalarGridSpec(
            num_scalar_prefetch=1,
            grid=(1,),
            in_specs=[pl.BlockSpec(memory_space=pl.ANY)] * (2 * SIDE),
            out_specs=[pl.BlockSpec(memory_space=pl.ANY)] * number,
            scratch_shapes=[
                pltpu.VMEM((2, SIDE - 1, *out.shape), jnp.bfloat16),
                pltpu.SemaphoreType.DMA((2, SIDE - 1, SIDE)),
                pltpu.SemaphoreType.DMA((2, SIDE - 1)),
            ],
        ),
        compiler_params=pltpu.CompilerParams(vmem_limit_bytes=VMEM),
        cost_estimate=pl.CostEstimate(
            flops=0, bytes_accessed=2 * number * SIDE * CAP * height * cols * 2, transcendentals=0
        ),
        name="regroup",
    )(begin, *lists)


def clear_kernel(count_ref, out_ref, zeros, sem):
    zeros[...] = jnp.zeros_like(zeros)
    height = zeros.shape[0]
    parts = out_ref.shape[1] // height

    def each(act):
        @pl.loop(count_ref[0], CAP)
        def _(slot):
            for part in range(parts):
                act(pltpu.make_async_copy(zeros, out_ref.at[slot, pl.ds(part * height, height)], sem))

    each(lambda c: c.start())
    each(lambda c: c.wait())


def clear(count, rows, cols):
    return pl.pallas_call(
        clear_kernel,
        out_shape=jax.ShapeDtypeStruct((CAP, rows, cols), jnp.bfloat16),
        grid_spec=pltpu.PrefetchScalarGridSpec(
            num_scalar_prefetch=1,
            grid=(1,),
            in_specs=[],
            out_specs=pl.BlockSpec(memory_space=pl.ANY),
            scratch_shapes=[pltpu.VMEM((rows // 2, cols), jnp.bfloat16), pltpu.SemaphoreType.DMA],
        ),
        compiler_params=pltpu.CompilerParams(vmem_limit_bytes=VMEM),
        cost_estimate=pl.CostEstimate(flops=0, bytes_accessed=CAP * rows * cols * 2, transcendentals=0),
        name="clear",
    )(count)


def unpack_kernel(chunk, meta_ref, *refs):
    own, others = refs[: 2 * SIDE], refs[2 * SIDE : -5]
    out_ref, held, got, put = refs[-4:]
    z, x = meta_ref[5], meta_ref[6]
    _, _, _, _, height, cols = held.shape
    width = out_ref.shape[2] // (SIDE * SIDE)
    places = [(half, r, k) for half in range(2) for r in range(SIDE) for k in range(SIDE)]
    ins = []
    for half in range(2):
        for k in range(SIDE):
            ins.append(pltpu.make_async_copy(
                own[half * SIDE + k].at[pl.ds(meta_ref[3 + half], CAP)], held.at[half, 0, k], got.at[half, k]
            ))
        for r in range(1, SIDE):
            ins.append(pltpu.make_async_copy(
                others[half * (SIDE - 1) + r - 1], held.at[half, r], got.at[half, SIDE + r - 1]
            ))
    for copy in ins:
        copy.start()
    for copy in ins:
        copy.wait()

    def each(bit, act):
        @pl.when(lax.rem(meta_ref[0], 2 * bit) >= bit)
        def _():
            before = meta_ref[0] - lax.rem(meta_ref[0], 2 * bit)
            for half, r, k in places:
                back_z, back_x = (k, r) if half == 0 else (r, k)
                source = lax.rem(z + SIDE - back_z, SIDE) * SIDE + lax.rem(x + SIDE - back_x, SIDE)
                at = pl.multiple_of(source * width + chunk * cols, cols)
                act(pltpu.make_async_copy(
                    held.at[half, r, k, pl.ds(meta_ref[1 + half] + before, bit)],
                    out_ref.at[pl.ds(before, bit), pl.ds(half * height, height), pl.ds(at, cols)],
                    put.at[bit.bit_length() - 1, half, r, k],
                ))

    for bit in (8, 4, 2, 1):
        each(bit, lambda c: c.start())
    for bit in (8, 4, 2, 1):
        each(bit, lambda c: c.wait())


def unpack(meta, own, others, chunk, before):
    height, cols = own[0].shape[-2:]

    def kernel(*refs):
        unpack_kernel(chunk, *refs)

    operands = [*own, *others, before]
    return pl.pallas_call(
        kernel,
        out_shape=jax.ShapeDtypeStruct(before.shape, before.dtype),
        grid_spec=pltpu.PrefetchScalarGridSpec(
            num_scalar_prefetch=1,
            grid=(1,),
            in_specs=[pl.BlockSpec(memory_space=pl.ANY)] * len(operands),
            out_specs=pl.BlockSpec(memory_space=pl.ANY),
            scratch_shapes=[
                pltpu.VMEM((2, SIDE, SIDE, CAP, height, cols), jnp.bfloat16),
                pltpu.SemaphoreType.DMA((2, 2 * SIDE - 1)),
                pltpu.SemaphoreType.DMA((4, 2, SIDE, SIDE)),
            ],
        ),
        input_output_aliases={len(operands): 0},
        compiler_params=pltpu.CompilerParams(vmem_limit_bytes=VMEM),
        cost_estimate=pl.CostEstimate(
            flops=0, bytes_accessed=2 * 2 * SIDE * SIDE * CAP * height * cols * 2, transcendentals=0
        ),
        name="unpack",
    )(meta, *operands)


def deliver(capacity, base, up, down_first, down_here, meta, begin, count, z, x, out):
    start = jnp.minimum(begin, capacity - CAP)
    skip = begin[:, 0] - start[:, 0]
    tail = jnp.stack([count, skip[0], skip[1], start[0, 0], start[1, 0], z, x])
    gathered = [down_first]
    for chunk in range(1, CHUNKS):
        gathered.append(gather(down_here, chunk))
    pending = []
    for chunk in range(CHUNKS):
        sends = merge(meta, base, up, gathered[chunk], chunk, capacity)
        lists = [None] * (2 * SIDE)
        for half in range(2):
            lists[half * SIDE] = sends[half * SIDE]
        for k in ORDER:
            for half in range(2):
                lists[half * SIDE + k] = send(sends[half * SIDE + k], half, True, k)
        pending.append(lists)
    for chunk, lists in enumerate(pending):
        groups = regroup(start, lists)
        others = [None] * (2 * (SIDE - 1))
        for r in ORDER:
            for half in range(2):
                others[half * (SIDE - 1) + r - 1] = send(groups[half * (SIDE - 1) + r - 1], half, False, r)
        out = unpack(tail, lists, others, chunk, out)
    return out


def gather(down_here, chunk):
    cols = down_here.shape[2] // CHUNKS
    return lax.all_gather(down_here[:, :, chunk * cols : (chunk + 1) * cols], "row", axis=1, tiled=True)


def body(base_weights, adapter_up_factor, adapter_down, file_sizes, file_writer):
    tensors = base_weights.shape[0] * base_weights.shape[1]
    base = base_weights.reshape(tensors, *base_weights.shape[2:])
    up = adapter_up_factor.reshape(tensors, *adapter_up_factor.shape[2:])
    down_here = adapter_down.reshape(tensors, *adapter_down.shape[2:])
    rank = lax.axis_index("expert")
    z, x = rank // SIDE, rank % SIDE
    meta, begin, count, most = route(file_sizes, file_writer, tensors, z, x)
    down = gather(down_here, 0)
    out = clear(count[None], base.shape[1], base.shape[2] * SIDE * SIDE)
    which = jnp.sum(most > jnp.array(CAPACITIES[:-1], jnp.int32)).astype(jnp.int32)
    branches = [lambda *a, c=c: deliver(c, *a) for c in CAPACITIES]
    return lax.switch(which, branches, base, up, down, down_here, meta, begin, count, z, x, out)


def solution(mesh):
    in_specs = (
        P(None, None, "row", "expert"),
        P(None, None, None, "row"),
        P(None, None, "row", "expert"),
        P(),
        P(),
    )
    out_specs = P("expert", "row", None)
    return jax.shard_map(body, mesh=mesh, in_specs=in_specs, out_specs=out_specs, check_vma=False)
```

```python
import jax
import jax.numpy as jnp
from jax import lax
from jax.experimental import pallas as pl
from jax.experimental.pallas import tpu as pltpu
from jax.sharding import PartitionSpec as P

CAP = 8
SIDE = 4
STEP = 8
CAPACITIES = (18, 20, 22, 24, 26, 32)
scaling = 0.125
VMEM = 60 * 1024 * 1024


def lines(first, rows):
    groups = []
    for row in range(rows):
        along_z = (row % 2 == 0) == first
        for at in range(SIDE):
            ranks = [(i * SIDE + at) if along_z else (at * SIDE + i) for i in range(SIDE)]
            groups.append([rank * rows + row for rank in ranks])
    return groups


def exchange(block, first):
    groups = lines(first, lax.axis_size("row"))
    return lax.all_to_all(block, ("expert", "row"), 0, 0, axis_index_groups=groups)


def route(file_sizes, file_writer, tensors, rank, core):
    files = file_sizes.shape[0]
    ids = jnp.arange(files, dtype=jnp.int32)
    starts = jnp.sum(jnp.where(ids[None, :] < ids[:, None], file_sizes[None, :], 0), axis=1)
    owns = file_writer[None, :] == ids[:, None]
    size_of = jnp.sum(jnp.where(owns, file_sizes[None, :], 0), axis=1)
    wz, wx = ids // SIDE, ids % SIDE
    in_row = (wz[:, None] == wz[None, :]) & (wx[None, :] < wx[:, None])
    in_col = (wx[:, None] == wx[None, :]) & (wz[None, :] < wz[:, None])
    first_row = jnp.sum(jnp.where(in_row, size_of[None, :], 0), axis=1)
    first_col = jnp.sum(jnp.where(in_col, size_of[None, :], 0), axis=1)
    most = jnp.maximum(jnp.max(first_row + size_of), jnp.max(first_col + size_of))
    even = core == 0
    first = jnp.where(even, first_row, first_col)
    f_of, g_of = jnp.where(even, wz, wx), jnp.where(even, wx, wz)

    number = jnp.arange(tensors, dtype=jnp.int32)[:, None]
    inside = (number >= starts[None, :]) & (number < (starts + file_sizes)[None, :])
    first_of_file = jnp.sum(jnp.where(owns, first[:, None], 0), axis=0)
    f_of_file = jnp.sum(jnp.where(owns, f_of[:, None], 0), axis=0)
    line = jnp.sum(jnp.where(inside, f_of_file[None, :], 0), axis=1)
    spot = jnp.sum(jnp.where(inside, (first_of_file - starts)[None, :] + number, 0), axis=1)
    mine = ids == rank
    here = f_of == jnp.sum(jnp.where(mine, f_of, 0))
    at = here[None, :] & (g_of[None, :] == jnp.arange(SIDE, dtype=jnp.int32)[:, None])
    begin = jnp.sum(jnp.where(at, first[None, :], 0), axis=1)
    size = jnp.sum(jnp.where(at, size_of[None, :], 0), axis=1)
    count = jnp.sum(jnp.where(mine, size_of, 0))
    ints = (jnp.concatenate([line, spot]), jnp.concatenate([begin, size]), jnp.stack([count, core]), most)
    return tuple(i.astype(jnp.int32) for i in ints)


def merge_kernel(capacity, place_ref, base_ref, up_ref, down_ref, out_ref, held, sems):
    step = pl.program_id(0)
    steps = pl.num_programs(0)
    slot = lax.rem(step, 2)

    def copy(slot, at, i):
        tensor = at * STEP + i
        place = place_ref[tensor] * capacity + place_ref[steps * STEP + tensor]
        return pltpu.make_async_copy(held.at[slot, i], out_ref.at[place], sems.at[slot, i])

    @pl.when(step >= 2)
    def _():
        for i in range(STEP):
            copy(slot, step - 2, i).wait()

    for i in range(STEP):
        delta = lax.dot_general(
            up_ref[i], down_ref[i], (((0,), (0,)), ((), ())), preferred_element_type=jnp.float32
        )
        held[slot, i] = (base_ref[i].astype(jnp.float32) + scaling * delta).astype(jnp.bfloat16)
        copy(slot, step, i).start()

    @pl.when(step == steps - 1)
    def _():
        for i in range(STEP):
            copy(1 - slot, step - 1, i).wait()
        for i in range(STEP):
            copy(slot, step, i).wait()


def merge(place, base, up, down, capacity):
    tensors, rows, cols = base.shape
    rank = up.shape[1]

    def kernel(*refs):
        merge_kernel(capacity, *refs)

    return pl.pallas_call(
        kernel,
        out_shape=jax.ShapeDtypeStruct((SIDE * capacity, rows, cols), jnp.bfloat16),
        grid_spec=pltpu.PrefetchScalarGridSpec(
            num_scalar_prefetch=1,
            grid=(tensors // STEP,),
            in_specs=[
                pl.BlockSpec((STEP, rows, cols), lambda s, p: (s, 0, 0)),
                pl.BlockSpec((STEP, rank, rows), lambda s, p: (s, 0, 0)),
                pl.BlockSpec((STEP, rank, cols), lambda s, p: (s, 0, 0)),
            ],
            out_specs=pl.BlockSpec(memory_space=pl.ANY),
            scratch_shapes=[
                pltpu.VMEM((2, STEP, rows, cols), jnp.bfloat16),
                pltpu.SemaphoreType.DMA((2, STEP)),
            ],
        ),
        compiler_params=pltpu.CompilerParams(vmem_limit_bytes=VMEM),
        name="merge",
    )(place, base, up, down)


def regroup_kernel(lists_ref, arrived_ref, out_ref, held, got, put):
    bits = (8, 4, 2, 1)

    def each(act):
        for g in range(SIDE):
            begin, size = lists_ref[g], lists_ref[SIDE + g]
            for b, bit in enumerate(bits):

                @pl.when(lax.rem(size, 2 * bit) >= bit)
                def _():
                    before = size - lax.rem(size, 2 * bit)
                    for k in range(SIDE):
                        slots = pl.ds(before, bit)
                        room = held.at[g, k, slots]
                        source = arrived_ref.at[k, pl.ds(begin + before, bit)]
                        act(
                            pltpu.make_async_copy(source, room, got.at[b, g, k]),
                            pltpu.make_async_copy(room, out_ref.at[g, k, slots], put.at[b, g, k]),
                        )

    def turn(come, leave):
        come.wait()
        leave.start()

    each(lambda come, leave: come.start())
    each(turn)
    each(lambda come, leave: leave.wait())


def regroup(lists, arrived):
    side, _, rows, cols = arrived.shape
    shape = (side, side, CAP, rows, cols)
    return pl.pallas_call(
        regroup_kernel,
        out_shape=jax.ShapeDtypeStruct(shape, jnp.bfloat16),
        grid_spec=pltpu.PrefetchScalarGridSpec(
            num_scalar_prefetch=1,
            grid=(1,),
            in_specs=[pl.BlockSpec(memory_space=pl.ANY)],
            out_specs=pl.BlockSpec(memory_space=pl.ANY),
            scratch_shapes=[
                pltpu.VMEM(shape, jnp.bfloat16),
                pltpu.SemaphoreType.DMA((4, side, side)),
                pltpu.SemaphoreType.DMA((4, side, side)),
            ],
        ),
        compiler_params=pltpu.CompilerParams(vmem_limit_bytes=VMEM),
        name="regroup",
    )(lists, arrived)


def unpack_kernel(meta_ref, arrived_ref, out_ref):
    slot = pl.program_id(0)
    cols = arrived_ref.shape[-1]
    for core in range(2):

        @pl.when((slot < meta_ref[0]) & (meta_ref[1] == core))
        def _():
            for g in range(SIDE):
                for f in range(SIDE):
                    source = f * SIDE + g if core == 0 else g * SIDE + f
                    out_ref[0, :, source * cols : (source + 1) * cols] = arrived_ref[g, f, 0]

    @pl.when(slot >= meta_ref[0])
    def _():
        out_ref[...] = jnp.zeros_like(out_ref)


def unpack(meta, arrived):
    side, _, slots, rows, cols = arrived.shape
    width = side * side * cols
    return pl.pallas_call(
        unpack_kernel,
        out_shape=jax.ShapeDtypeStruct((slots, rows, width), jnp.bfloat16),
        grid_spec=pltpu.PrefetchScalarGridSpec(
            num_scalar_prefetch=1,
            grid=(slots,),
            in_specs=[
                pl.BlockSpec((side, side, 1, rows, cols), lambda s, m: (0, 0, jnp.minimum(s, m[0] - 1), 0, 0))
            ],
            out_specs=pl.BlockSpec((1, rows, width), lambda s, m: (s, 0, 0)),
        ),
        compiler_params=pltpu.CompilerParams(vmem_limit_bytes=VMEM),
        name="unpack",
    )(meta, arrived)


def to_lines(capacity, place, lists, base, up, down):
    sends = merge(place, base, up, down, capacity)
    arrived = exchange(sends.reshape(SIDE, capacity, *sends.shape[1:]), True)
    return regroup(lists, arrived)


def body(base_weights, adapter_up_factor, adapter_down, file_sizes, file_writer):
    tensors = base_weights.shape[0] * base_weights.shape[1]
    base = base_weights.reshape(tensors, *base_weights.shape[2:])
    up = adapter_up_factor.reshape(tensors, *adapter_up_factor.shape[2:])
    down_here = adapter_down.reshape(tensors, *adapter_down.shape[2:])
    place, lists, meta, most = route(
        file_sizes, file_writer, tensors, lax.axis_index("expert"), lax.axis_index("row") % 2
    )
    which = jnp.sum(most > jnp.array(CAPACITIES[:-1], jnp.int32)).astype(jnp.int32)
    down = lax.all_gather(down_here, "row", axis=1, tiled=True)
    branches = [lambda *a, c=c: to_lines(c, *a) for c in CAPACITIES]
    groups = lax.switch(which, branches, place, lists, base, up, down)
    groups, meta = lax.optimization_barrier((groups, meta))
    return unpack(meta, exchange(groups, False))


def solution(mesh):
    in_specs = (
        P(None, None, "row", "expert"),
        P(None, None, None, "row"),
        P(None, None, "row", "expert"),
        P(),
        P(),
    )
    out_specs = P("expert", "row", None)
    return jax.shard_map(body, mesh=mesh, in_specs=in_specs, out_specs=out_specs, check_vma=False)
```

```python
import jax
import jax.numpy as jnp
from jax import lax
from jax.experimental import pallas as pl
from jax.experimental.pallas import tpu as pltpu
from jax.sharding import PartitionSpec as P

CAP = 8
SIDE = 4
Y = 4
STEP = 8
CAPACITIES = (18, 20, 22, 24, 26, 32)
scaling = 0.125
VMEM = 16 * 1024 * 1024


def lines(first, rows):
    groups = []
    for row in range(rows):
        along_z = (row % 2 == 0) == first
        for at in range(SIDE):
            ranks = [(i * SIDE + at) if along_z else (at * SIDE + i) for i in range(SIDE)]
            groups.append([rank * rows + row for rank in ranks])
    return groups


def exchange(block, first):
    groups = lines(first, lax.axis_size("row"))
    return lax.all_to_all(block, ("expert", "row"), 0, 0, axis_index_groups=groups)


def route(file_sizes, file_writer, tensors, rank, core):
    files = file_sizes.shape[0]
    ids = jnp.arange(files, dtype=jnp.int32)
    starts = jnp.sum(jnp.where(ids[None, :] < ids[:, None], file_sizes[None, :], 0), axis=1)
    owns = file_writer[None, :] == ids[:, None]
    size_of = jnp.sum(jnp.where(owns, file_sizes[None, :], 0), axis=1)
    wz, wx = ids // SIDE, ids % SIDE
    in_row = (wz[:, None] == wz[None, :]) & (wx[None, :] < wx[:, None])
    in_col = (wx[:, None] == wx[None, :]) & (wz[None, :] < wz[:, None])
    first_row = jnp.sum(jnp.where(in_row, size_of[None, :], 0), axis=1)
    first_col = jnp.sum(jnp.where(in_col, size_of[None, :], 0), axis=1)
    most = jnp.maximum(jnp.max(first_row + size_of), jnp.max(first_col + size_of))
    even = core == 0
    first = jnp.where(even, first_row, first_col)
    f_of, g_of = jnp.where(even, wz, wx), jnp.where(even, wx, wz)

    number = jnp.arange(tensors, dtype=jnp.int32)[:, None]
    inside = (number >= starts[None, :]) & (number < (starts + file_sizes)[None, :])
    first_of_file = jnp.sum(jnp.where(owns, first[:, None], 0), axis=0)
    f_of_file = jnp.sum(jnp.where(owns, f_of[:, None], 0), axis=0)
    line = jnp.sum(jnp.where(inside, f_of_file[None, :], 0), axis=1)
    spot = jnp.sum(jnp.where(inside, (first_of_file - starts)[None, :] + number, 0), axis=1)
    mine = ids == rank
    here = f_of == jnp.sum(jnp.where(mine, f_of, 0))
    at = here[None, :] & (g_of[None, :] == jnp.arange(SIDE, dtype=jnp.int32)[:, None])
    begin = jnp.sum(jnp.where(at, first[None, :], 0), axis=1)
    size = jnp.sum(jnp.where(at, size_of[None, :], 0), axis=1)
    count = jnp.sum(jnp.where(mine, size_of, 0))
    ints = (jnp.concatenate([line, spot]), jnp.concatenate([begin, size]), jnp.stack([count, core]), most)
    return tuple(i.astype(jnp.int32) for i in ints)


def merge_kernel(capacity, place_ref, at_ref, base_ref, *rest):
    ups, downs, (out_ref, held, sems) = rest[:Y], rest[Y : 3 * Y], rest[3 * Y :]
    step = pl.program_id(0)
    steps = pl.num_programs(0)
    slot = lax.rem(step, 2)
    even = at_ref[1] == 0

    def copy(slot, at, i):
        tensor = at * STEP + i
        place = place_ref[tensor] * capacity + place_ref[steps * STEP + tensor]
        return pltpu.make_async_copy(held.at[slot, i], out_ref.at[place], sems.at[slot, i])

    @pl.when(step >= 2)
    def _():
        for i in range(STEP):
            copy(slot, step - 2, i).wait()

    for i in range(STEP):
        up = jnp.concatenate([ref[i] for ref in ups], axis=0)
        parts = []
        for k in range(Y):
            same, other = downs[k][i].astype(jnp.float32), downs[Y + k][i].astype(jnp.float32)
            parts += [jnp.where(even, same, other), jnp.where(even, other, same)]
        down = jnp.concatenate(parts, axis=0).astype(jnp.bfloat16)
        delta = lax.dot_general(up, down, (((0,), (0,)), ((), ())), preferred_element_type=jnp.float32)
        held[slot, i] = (base_ref[i].astype(jnp.float32) + scaling * delta).astype(jnp.bfloat16)
        copy(slot, step, i).start()

    @pl.when(step == steps - 1)
    def _():
        for i in range(STEP):
            copy(1 - slot, step - 1, i).wait()
        for i in range(STEP):
            copy(slot, step, i).wait()


def merge(place, at, base, up, downs, capacity):
    tensors, rows, cols = base.shape
    rank = up.shape[1]
    share = rank // (2 * Y)

    def kernel(*refs):
        merge_kernel(capacity, *refs)

    return pl.pallas_call(
        kernel,
        out_shape=jax.ShapeDtypeStruct((SIDE * capacity, rows, cols), jnp.bfloat16),
        grid_spec=pltpu.PrefetchScalarGridSpec(
            num_scalar_prefetch=2,
            grid=(tensors // STEP,),
            in_specs=[
                pl.BlockSpec((STEP, rows, cols), lambda s, p, a: (s, 0, 0)),
                *[
                    pl.BlockSpec((STEP, 2 * share, rows), lambda s, p, a, k=k: (s, lax.rem(a[0] + Y - k, Y), 0))
                    for k in range(Y)
                ],
                *[pl.BlockSpec((STEP, share, cols), lambda s, p, a: (s, 0, 0))] * (2 * Y),
            ],
            out_specs=pl.BlockSpec(memory_space=pl.ANY),
            scratch_shapes=[
                pltpu.VMEM((2, STEP, rows, cols), jnp.bfloat16),
                pltpu.SemaphoreType.DMA((2, STEP)),
            ],
        ),
        compiler_params=pltpu.CompilerParams(vmem_limit_bytes=VMEM),
        name="merge",
    )(place, at, base, *[up] * Y, *downs)


def gather(down_here):
    around = [down_here]
    for k in (1, 3, 2):
        pairs = [(y * 2 + c, (y + k) % Y * 2 + c) for y in range(Y) for c in range(2)]
        around.append(lax.ppermute(down_here, "row", pairs))
    around = [around[0], around[1], around[3], around[2]]
    other = [lax.ppermute(part, "row", [(row, row ^ 1) for row in range(2 * Y)]) for part in around]
    return around + other


def regroup_kernel(lists_ref, arrived_ref, out_ref, sems):
    def each(act):
        for g in range(SIDE):
            begin, size = lists_ref[g], lists_ref[SIDE + g]
            for b, bit in enumerate((8, 4, 2, 1)):

                @pl.when(lax.rem(size, 2 * bit) >= bit)
                def _():
                    before = size - lax.rem(size, 2 * bit)
                    for k in range(SIDE):
                        source = arrived_ref.at[k, pl.ds(begin + before, bit)]
                        act(pltpu.make_async_copy(source, out_ref.at[g, k, pl.ds(before, bit)], sems.at[b, g, k]))

    each(lambda c: c.start())
    each(lambda c: c.wait())


def regroup(lists, arrived):
    side, _, rows, cols = arrived.shape
    return pl.pallas_call(
        regroup_kernel,
        out_shape=jax.ShapeDtypeStruct((side, side, CAP, rows, cols), jnp.bfloat16),
        grid_spec=pltpu.PrefetchScalarGridSpec(
            num_scalar_prefetch=1,
            grid=(1,),
            in_specs=[pl.BlockSpec(memory_space=pl.ANY)],
            out_specs=pl.BlockSpec(memory_space=pl.ANY),
            scratch_shapes=[pltpu.SemaphoreType.DMA((4, side, side))],
        ),
        compiler_params=pltpu.CompilerParams(vmem_limit_bytes=VMEM),
        name="regroup",
    )(lists, arrived)


def unpack_kernel(meta_ref, arrived_ref, out_ref):
    slot = pl.program_id(0)
    cols = arrived_ref.shape[-1]
    for core in range(2):

        @pl.when((slot < meta_ref[0]) & (meta_ref[1] == core))
        def _():
            for g in range(SIDE):
                for f in range(SIDE):
                    source = f * SIDE + g if core == 0 else g * SIDE + f
                    out_ref[0, :, source * cols : (source + 1) * cols] = arrived_ref[g, f, 0]

    @pl.when(slot >= meta_ref[0])
    def _():
        out_ref[...] = jnp.zeros_like(out_ref)


def unpack(meta, arrived):
    side, _, slots, rows, cols = arrived.shape
    width = side * side * cols
    return pl.pallas_call(
        unpack_kernel,
        out_shape=jax.ShapeDtypeStruct((slots, rows, width), jnp.bfloat16),
        grid_spec=pltpu.PrefetchScalarGridSpec(
            num_scalar_prefetch=1,
            grid=(slots,),
            in_specs=[
                pl.BlockSpec((side, side, 1, rows, cols), lambda s, m: (0, 0, jnp.minimum(s, m[0] - 1), 0, 0))
            ],
            out_specs=pl.BlockSpec((1, rows, width), lambda s, m: (s, 0, 0)),
        ),
        compiler_params=pltpu.CompilerParams(vmem_limit_bytes=VMEM),
        name="unpack",
    )(meta, arrived)


def to_lines(capacity, place, at, lists, base, up, downs):
    sends = merge(place, at, base, up, downs, capacity)
    arrived = exchange(sends.reshape(SIDE, capacity, *sends.shape[1:]), True)
    return regroup(lists, arrived)


def body(base_weights, adapter_up_factor, adapter_down, file_sizes, file_writer):
    tensors = base_weights.shape[0] * base_weights.shape[1]
    base = base_weights.reshape(tensors, *base_weights.shape[2:])
    up = adapter_up_factor.reshape(tensors, *adapter_up_factor.shape[2:])
    down_here = adapter_down.reshape(tensors, *adapter_down.shape[2:])
    place, lists, meta, most = route(
        file_sizes, file_writer, tensors, lax.axis_index("expert"), lax.axis_index("row") % 2
    )
    which = jnp.sum(most > jnp.array(CAPACITIES[:-1], jnp.int32)).astype(jnp.int32)
    downs = gather(down_here)
    row = lax.axis_index("row")
    at = jnp.stack([row // 2, row % 2]).astype(jnp.int32)
    branches = [lambda *a, c=c: to_lines(c, *a) for c in CAPACITIES]
    groups = lax.switch(which, branches, place, at, lists, base, up, downs)
    groups, meta = lax.optimization_barrier((groups, meta))
    return unpack(meta, exchange(groups, False))


def solution(mesh):
    in_specs = (
        P(None, None, "row", "expert"),
        P(None, None, None, "row"),
        P(None, None, "row", "expert"),
        P(),
        P(),
    )
    out_specs = P("expert", "row", None)
    return jax.shard_map(body, mesh=mesh, in_specs=in_specs, out_specs=out_specs, check_vma=False)
```

```python
import jax
import jax.numpy as jnp
from jax import lax
from jax.experimental import pallas as pl
from jax.experimental.pallas import tpu as pltpu
from jax.sharding import PartitionSpec as P

CAP = 8
SIDE = 4
Y = 4
STEP = 8
CAPACITIES = (18, 20, 21, 22, 23, 24, 25, 26, 28, 32)
scaling = 0.125
VMEM = 16 * 1024 * 1024


def lines(first, rows):
    groups = []
    for row in range(rows):
        along_z = (row % 2 == 0) == first
        for at in range(SIDE):
            ranks = [(i * SIDE + at) if along_z else (at * SIDE + i) for i in range(SIDE)]
            groups.append([rank * rows + row for rank in ranks])
    return groups


def exchange(block, first):
    groups = lines(first, lax.axis_size("row"))
    return lax.all_to_all(block, ("expert", "row"), 0, 0, axis_index_groups=groups)


def route(file_sizes, file_writer, tensors, rank, core):
    files = file_sizes.shape[0]
    ids = jnp.arange(files, dtype=jnp.int32)
    starts = jnp.sum(jnp.where(ids[None, :] < ids[:, None], file_sizes[None, :], 0), axis=1)
    owns = file_writer[None, :] == ids[:, None]
    size_of = jnp.sum(jnp.where(owns, file_sizes[None, :], 0), axis=1)
    wz, wx = ids // SIDE, ids % SIDE
    in_row = (wz[:, None] == wz[None, :]) & (wx[None, :] < wx[:, None])
    in_col = (wx[:, None] == wx[None, :]) & (wz[None, :] < wz[:, None])
    first_row = jnp.sum(jnp.where(in_row, size_of[None, :], 0), axis=1)
    first_col = jnp.sum(jnp.where(in_col, size_of[None, :], 0), axis=1)
    most = jnp.maximum(jnp.max(first_row + size_of), jnp.max(first_col + size_of))
    even = core == 0
    first = jnp.where(even, first_row, first_col)
    f_of, g_of = jnp.where(even, wz, wx), jnp.where(even, wx, wz)

    number = jnp.arange(tensors, dtype=jnp.int32)[:, None]
    inside = (number >= starts[None, :]) & (number < (starts + file_sizes)[None, :])
    first_of_file = jnp.sum(jnp.where(owns, first[:, None], 0), axis=0)
    f_of_file = jnp.sum(jnp.where(owns, f_of[:, None], 0), axis=0)
    line = jnp.sum(jnp.where(inside, f_of_file[None, :], 0), axis=1)
    spot = jnp.sum(jnp.where(inside, (first_of_file - starts)[None, :] + number, 0), axis=1)
    mine = ids == rank
    here = f_of == jnp.sum(jnp.where(mine, f_of, 0))
    at = here[None, :] & (g_of[None, :] == jnp.arange(SIDE, dtype=jnp.int32)[:, None])
    begin = jnp.sum(jnp.where(at, first[None, :], 0), axis=1)
    size = jnp.sum(jnp.where(at, size_of[None, :], 0), axis=1)
    count = jnp.sum(jnp.where(mine, size_of, 0))
    ints = (jnp.concatenate([line, spot]), jnp.concatenate([begin, size]), jnp.stack([count, core]), most)
    return tuple(i.astype(jnp.int32) for i in ints)


def merge_kernel(capacity, place_ref, base_ref, up_ref, down_ref, out_ref, held, sems):
    step = pl.program_id(0)
    steps = pl.num_programs(0)
    slot = lax.rem(step, 2)

    def copy(slot, at, i):
        tensor = at * STEP + i
        place = place_ref[tensor] * capacity + place_ref[steps * STEP + tensor]
        return pltpu.make_async_copy(held.at[slot, i], out_ref.at[place], sems.at[slot, i])

    @pl.when(step >= 2)
    def _():
        for i in range(STEP):
            copy(slot, step - 2, i).wait()

    for i in range(STEP):
        delta = lax.dot_general(
            up_ref[i], down_ref[i], (((0,), (0,)), ((), ())), preferred_element_type=jnp.float32
        )
        held[slot, i] = (base_ref[i].astype(jnp.float32) + scaling * delta).astype(jnp.bfloat16)
        copy(slot, step, i).start()

    @pl.when(step == steps - 1)
    def _():
        for i in range(STEP):
            copy(1 - slot, step - 1, i).wait()
        for i in range(STEP):
            copy(slot, step, i).wait()


def merge(place, base, up, down, capacity):
    tensors, rows, cols = base.shape
    rank = up.shape[1]

    def kernel(*refs):
        merge_kernel(capacity, *refs)

    return pl.pallas_call(
        kernel,
        out_shape=jax.ShapeDtypeStruct((SIDE * capacity, rows, cols), jnp.bfloat16),
        grid_spec=pltpu.PrefetchScalarGridSpec(
            num_scalar_prefetch=1,
            grid=(tensors // STEP,),
            in_specs=[
                pl.BlockSpec((STEP, rows, cols), lambda s, p: (s, 0, 0)),
                pl.BlockSpec((STEP, rank, rows), lambda s, p: (s, 0, 0)),
                pl.BlockSpec((STEP, rank, cols), lambda s, p: (s, 0, 0)),
            ],
            out_specs=pl.BlockSpec(memory_space=pl.ANY),
            scratch_shapes=[
                pltpu.VMEM((2, STEP, rows, cols), jnp.bfloat16),
                pltpu.SemaphoreType.DMA((2, STEP)),
            ],
        ),
        compiler_params=pltpu.CompilerParams(vmem_limit_bytes=VMEM),
        name="merge",
    )(place, base, up, down)


def gather(down_here, row):
    tensors, share, cols = down_here.shape
    y, core = row // 2, row % 2
    whole = jnp.zeros((tensors, 2 * Y, share, cols), down_here.dtype)

    def put(whole, part, k, of_core):
        block = (y + Y - k) % Y * 2 + of_core
        return lax.dynamic_update_slice(whole, part[:, None], (0, block, 0, 0))

    around = {0: down_here}
    for k in (1, 3, 2):
        pairs = [(at * 2 + c, (at + k) % Y * 2 + c) for at in range(Y) for c in range(2)]
        around[k] = lax.ppermute(down_here, "row", pairs)
    for k in (0, 1, 3, 2):
        other = lax.ppermute(around[k], "row", [(at, at ^ 1) for at in range(2 * Y)])
        whole = put(put(whole, around[k], k, core), other, k, 1 - core)
    return whole.reshape(tensors, 2 * Y * share, cols)


def regroup_kernel(lists_ref, arrived_ref, out_ref, sems):
    def each(act):
        for g in range(SIDE):
            begin, size = lists_ref[g], lists_ref[SIDE + g]
            for b, bit in enumerate((8, 4, 2, 1)):

                @pl.when(lax.rem(size, 2 * bit) >= bit)
                def _():
                    before = size - lax.rem(size, 2 * bit)
                    for k in range(SIDE):
                        source = arrived_ref.at[k, pl.ds(begin + before, bit)]
                        act(pltpu.make_async_copy(source, out_ref.at[g, k, pl.ds(before, bit)], sems.at[b, g, k]))

    each(lambda c: c.start())
    each(lambda c: c.wait())


def regroup(lists, arrived):
    side, _, rows, cols = arrived.shape
    return pl.pallas_call(
        regroup_kernel,
        out_shape=jax.ShapeDtypeStruct((side, side, CAP, rows, cols), jnp.bfloat16),
        grid_spec=pltpu.PrefetchScalarGridSpec(
            num_scalar_prefetch=1,
            grid=(1,),
            in_specs=[pl.BlockSpec(memory_space=pl.ANY)],
            out_specs=pl.BlockSpec(memory_space=pl.ANY),
            scratch_shapes=[pltpu.SemaphoreType.DMA((4, side, side))],
        ),
        compiler_params=pltpu.CompilerParams(vmem_limit_bytes=VMEM),
        name="regroup",
    )(lists, arrived)


def unpack_kernel(meta_ref, arrived_ref, out_ref):
    slot = pl.program_id(0)
    cols = arrived_ref.shape[-1]
    for core in range(2):

        @pl.when((slot < meta_ref[0]) & (meta_ref[1] == core))
        def _():
            for g in range(SIDE):
                for f in range(SIDE):
                    source = f * SIDE + g if core == 0 else g * SIDE + f
                    out_ref[0, :, source * cols : (source + 1) * cols] = arrived_ref[g, f, 0]

    @pl.when(slot >= meta_ref[0])
    def _():
        out_ref[...] = jnp.zeros_like(out_ref)


def unpack(meta, arrived):
    side, _, slots, rows, cols = arrived.shape
    width = side * side * cols
    return pl.pallas_call(
        unpack_kernel,
        out_shape=jax.ShapeDtypeStruct((slots, rows, width), jnp.bfloat16),
        grid_spec=pltpu.PrefetchScalarGridSpec(
            num_scalar_prefetch=1,
            grid=(slots,),
            in_specs=[
                pl.BlockSpec((side, side, 1, rows, cols), lambda s, m: (0, 0, jnp.minimum(s, m[0] - 1), 0, 0))
            ],
            out_specs=pl.BlockSpec((1, rows, width), lambda s, m: (s, 0, 0)),
        ),
        compiler_params=pltpu.CompilerParams(vmem_limit_bytes=VMEM),
        name="unpack",
    )(meta, arrived)


def to_lines(capacity, place, lists, base, up, down):
    sends = merge(place, base, up, down, capacity)
    arrived = exchange(sends.reshape(SIDE, capacity, *sends.shape[1:]), True)
    return regroup(lists, arrived)


def body(base_weights, adapter_up_factor, adapter_down, file_sizes, file_writer):
    tensors = base_weights.shape[0] * base_weights.shape[1]
    base = base_weights.reshape(tensors, *base_weights.shape[2:])
    up = adapter_up_factor.reshape(tensors, *adapter_up_factor.shape[2:])
    down_here = adapter_down.reshape(tensors, *adapter_down.shape[2:])
    place, lists, meta, most = route(
        file_sizes, file_writer, tensors, lax.axis_index("expert"), lax.axis_index("row") % 2
    )
    which = jnp.sum(most > jnp.array(CAPACITIES[:-1], jnp.int32)).astype(jnp.int32)
    down = gather(down_here, lax.axis_index("row"))
    branches = [lambda *a, c=c: to_lines(c, *a) for c in CAPACITIES]
    groups = lax.switch(which, branches, place, lists, base, up, down)
    groups, meta = lax.optimization_barrier((groups, meta))
    return unpack(meta, exchange(groups, False))


def solution(mesh):
    in_specs = (
        P(None, None, "row", "expert"),
        P(None, None, None, "row"),
        P(None, None, "row", "expert"),
        P(),
        P(),
    )
    out_specs = P("expert", "row", None)
    return jax.shard_map(body, mesh=mesh, in_specs=in_specs, out_specs=out_specs, check_vma=False)
```

```python
import jax
import jax.numpy as jnp
from jax import lax
from jax.experimental import pallas as pl
from jax.experimental.pallas import tpu as pltpu
from jax.sharding import PartitionSpec as P

CAP = 8
SIDE = 4
Y = 4
STEP = 8
CAPACITIES = (18, 20, 21, 22, 23, 24, 25, 26, 28, 32)
scaling = 0.125
VMEM = 16 * 1024 * 1024


def lines(first, rows):
    groups = []
    for row in range(rows):
        along_z = (row % 2 == 0) == first
        for at in range(SIDE):
            ranks = [(i * SIDE + at) if along_z else (at * SIDE + i) for i in range(SIDE)]
            groups.append([rank * rows + row for rank in ranks])
    return groups


def exchange(block, first):
    groups = lines(first, lax.axis_size("row"))
    return lax.all_to_all(block, ("expert", "row"), 0, 0, axis_index_groups=groups)


def route(file_sizes, file_writer, tensors, rank, core):
    files = file_sizes.shape[0]
    ids = jnp.arange(files, dtype=jnp.int32)
    starts = jnp.sum(jnp.where(ids[None, :] < ids[:, None], file_sizes[None, :], 0), axis=1)
    owns = file_writer[None, :] == ids[:, None]
    size_of = jnp.sum(jnp.where(owns, file_sizes[None, :], 0), axis=1)
    wz, wx = ids // SIDE, ids % SIDE
    in_row = (wz[:, None] == wz[None, :]) & (wx[None, :] < wx[:, None])
    in_col = (wx[:, None] == wx[None, :]) & (wz[None, :] < wz[:, None])
    first_row = jnp.sum(jnp.where(in_row, size_of[None, :], 0), axis=1)
    first_col = jnp.sum(jnp.where(in_col, size_of[None, :], 0), axis=1)
    most = jnp.maximum(jnp.max(first_row + size_of), jnp.max(first_col + size_of))
    even = core == 0
    first = jnp.where(even, first_row, first_col)
    f_of, g_of = jnp.where(even, wz, wx), jnp.where(even, wx, wz)

    number = jnp.arange(tensors, dtype=jnp.int32)[:, None]
    inside = (number >= starts[None, :]) & (number < (starts + file_sizes)[None, :])
    first_of_file = jnp.sum(jnp.where(owns, first[:, None], 0), axis=0)
    f_of_file = jnp.sum(jnp.where(owns, f_of[:, None], 0), axis=0)
    line = jnp.sum(jnp.where(inside, f_of_file[None, :], 0), axis=1)
    spot = jnp.sum(jnp.where(inside, (first_of_file - starts)[None, :] + number, 0), axis=1)
    mine = ids == rank
    here = f_of == jnp.sum(jnp.where(mine, f_of, 0))
    at = here[None, :] & (g_of[None, :] == jnp.arange(SIDE, dtype=jnp.int32)[:, None])
    begin = jnp.sum(jnp.where(at, first[None, :], 0), axis=1)
    size = jnp.sum(jnp.where(at, size_of[None, :], 0), axis=1)
    count = jnp.sum(jnp.where(mine, size_of, 0))
    ints = (jnp.concatenate([line, spot]), jnp.concatenate([begin, size]), jnp.stack([count, core]), most)
    return tuple(i.astype(jnp.int32) for i in ints)


def merge_kernel(capacity, place_ref, base_ref, up_ref, down_ref, out_ref, held, held_up, sems):
    tensors = held.shape[0]
    steps = tensors // STEP

    def fetch(step):
        part = pl.ds(step * STEP, STEP)
        yield pltpu.make_async_copy(up_ref.at[part], held_up.at[part], sems.at[0, step])
        yield pltpu.make_async_copy(base_ref.at[part], held.at[part], sems.at[1, step])

    for step in range(steps):
        for copy in fetch(step):
            copy.start()

    @pl.loop(0, steps)
    def _(step):
        for copy in fetch(step):
            copy.wait()
        for i in range(STEP):
            tensor = step * STEP + i
            delta = lax.dot_general(
                held_up[tensor], down_ref[tensor], (((0,), (0,)), ((), ())), preferred_element_type=jnp.float32
            )
            merged = held[tensor].astype(jnp.float32) + scaling * delta
            out_ref[place_ref[tensor] * capacity + place_ref[tensors + tensor]] = merged.astype(jnp.bfloat16)


def merge(place, base, up, down, capacity):
    tensors, rows, cols = base.shape

    def kernel(*refs):
        merge_kernel(capacity, *refs)

    return pl.pallas_call(
        kernel,
        out_shape=jax.ShapeDtypeStruct((SIDE * capacity, rows, cols), jnp.bfloat16),
        in_specs=[
            pl.BlockSpec(memory_space=pltpu.SMEM),
            pl.BlockSpec(memory_space=pl.ANY),
            pl.BlockSpec(memory_space=pl.ANY),
            pl.BlockSpec(memory_space=pltpu.VMEM),
        ],
        out_specs=pl.BlockSpec(memory_space=pltpu.VMEM),
        scratch_shapes=[
            pltpu.VMEM((tensors, rows, cols), jnp.bfloat16),
            pltpu.VMEM((tensors, up.shape[1], rows), jnp.bfloat16),
            pltpu.SemaphoreType.DMA((2, tensors // STEP)),
        ],
        compiler_params=pltpu.CompilerParams(vmem_limit_bytes=2 * VMEM),
        name="merge",
    )(place, base, up, down)


def gather(down_here, row):
    tensors, share, cols = down_here.shape
    y, core = row // 2, row % 2
    whole = jnp.zeros((tensors, 2 * Y, share, cols), down_here.dtype)

    def put(whole, part, k, of_core):
        block = (y + Y - k) % Y * 2 + of_core
        return lax.dynamic_update_slice(whole, part[:, None], (0, block, 0, 0))

    around = {0: down_here}
    for k in (1, 3, 2):
        pairs = [(at * 2 + c, (at + k) % Y * 2 + c) for at in range(Y) for c in range(2)]
        around[k] = lax.ppermute(down_here, "row", pairs)
    for k in (0, 1, 3, 2):
        other = lax.ppermute(around[k], "row", [(at, at ^ 1) for at in range(2 * Y)])
        whole = put(put(whole, around[k], k, core), other, k, 1 - core)
    return whole.reshape(tensors, 2 * Y * share, cols)


def regroup_kernel(lists_ref, arrived_ref, out_ref, sems):
    def each(act):
        for g in range(SIDE):
            begin, size = lists_ref[g], lists_ref[SIDE + g]
            for b, bit in enumerate((8, 4, 2, 1)):

                @pl.when(lax.rem(size, 2 * bit) >= bit)
                def _():
                    before = size - lax.rem(size, 2 * bit)
                    for k in range(SIDE):
                        source = arrived_ref.at[k, pl.ds(begin + before, bit)]
                        act(pltpu.make_async_copy(source, out_ref.at[g, k, pl.ds(before, bit)], sems.at[b, g, k]))

    each(lambda c: c.start())
    each(lambda c: c.wait())


def regroup(lists, arrived):
    side, _, rows, cols = arrived.shape
    return pl.pallas_call(
        regroup_kernel,
        out_shape=jax.ShapeDtypeStruct((side, side, CAP, rows, cols), jnp.bfloat16),
        grid_spec=pltpu.PrefetchScalarGridSpec(
            num_scalar_prefetch=1,
            grid=(1,),
            in_specs=[pl.BlockSpec(memory_space=pl.ANY)],
            out_specs=pl.BlockSpec(memory_space=pl.ANY),
            scratch_shapes=[pltpu.SemaphoreType.DMA((4, side, side))],
        ),
        compiler_params=pltpu.CompilerParams(vmem_limit_bytes=VMEM),
        name="regroup",
    )(lists, arrived)


def unpack_kernel(meta_ref, arrived_ref, out_ref):
    slot = pl.program_id(0)
    cols = arrived_ref.shape[-1]
    for core in range(2):

        @pl.when((slot < meta_ref[0]) & (meta_ref[1] == core))
        def _():
            for g in range(SIDE):
                for f in range(SIDE):
                    source = f * SIDE + g if core == 0 else g * SIDE + f
                    out_ref[0, :, source * cols : (source + 1) * cols] = arrived_ref[g, f, 0]

    @pl.when(slot >= meta_ref[0])
    def _():
        out_ref[...] = jnp.zeros_like(out_ref)


def unpack(meta, arrived):
    side, _, slots, rows, cols = arrived.shape
    width = side * side * cols
    return pl.pallas_call(
        unpack_kernel,
        out_shape=jax.ShapeDtypeStruct((slots, rows, width), jnp.bfloat16),
        grid_spec=pltpu.PrefetchScalarGridSpec(
            num_scalar_prefetch=1,
            grid=(slots,),
            in_specs=[
                pl.BlockSpec((side, side, 1, rows, cols), lambda s, m: (0, 0, jnp.minimum(s, m[0] - 1), 0, 0))
            ],
            out_specs=pl.BlockSpec((1, rows, width), lambda s, m: (s, 0, 0)),
        ),
        compiler_params=pltpu.CompilerParams(vmem_limit_bytes=VMEM),
        name="unpack",
    )(meta, arrived)


def to_lines(capacity, place, lists, base, up, down):
    sends = merge(place, base, up, down, capacity)
    arrived = exchange(sends.reshape(SIDE, capacity, *sends.shape[1:]), True)
    return regroup(lists, arrived)


def body(base_weights, adapter_up_factor, adapter_down, file_sizes, file_writer):
    tensors = base_weights.shape[0] * base_weights.shape[1]
    base = base_weights.reshape(tensors, *base_weights.shape[2:])
    up = adapter_up_factor.reshape(tensors, *adapter_up_factor.shape[2:])
    down_here = adapter_down.reshape(tensors, *adapter_down.shape[2:])
    place, lists, meta, most = route(
        file_sizes, file_writer, tensors, lax.axis_index("expert"), lax.axis_index("row") % 2
    )
    which = jnp.sum(most > jnp.array(CAPACITIES[:-1], jnp.int32)).astype(jnp.int32)
    down = gather(down_here, lax.axis_index("row"))
    branches = [lambda *a, c=c: to_lines(c, *a) for c in CAPACITIES]
    groups = lax.switch(which, branches, place, lists, base, up, down)
    groups, meta = lax.optimization_barrier((groups, meta))
    return unpack(meta, exchange(groups, False))


def solution(mesh):
    in_specs = (
        P(None, None, "row", "expert"),
        P(None, None, None, "row"),
        P(None, None, "row", "expert"),
        P(),
        P(),
    )
    out_specs = P("expert", "row", None)
    return jax.shard_map(body, mesh=mesh, in_specs=in_specs, out_specs=out_specs, check_vma=False)
```

```python
import jax
import jax.numpy as jnp
from jax import lax
from jax.experimental import pallas as pl
from jax.experimental.pallas import tpu as pltpu
from jax.sharding import PartitionSpec as P

CAP = 8
SIDE = 4
Y = 4
STEP = 8
CAPACITIES = (18, 19, 20, 21, 22, 23, 24, 25, 26, 27, 28, 30, 32)
scaling = 0.125
VMEM = 16 * 1024 * 1024


def lines(first, rows):
    groups = []
    for row in range(rows):
        along_z = (row % 2 == 0) == first
        for at in range(SIDE):
            ranks = [(i * SIDE + at) if along_z else (at * SIDE + i) for i in range(SIDE)]
            groups.append([rank * rows + row for rank in ranks])
    return groups


def exchange(block, first):
    groups = lines(first, lax.axis_size("row"))
    return lax.all_to_all(block, ("expert", "row"), 0, 0, axis_index_groups=groups)


def route(file_sizes, file_writer, tensors, rank, core):
    files = file_sizes.shape[0]
    ids = jnp.arange(files, dtype=jnp.int32)
    starts = jnp.sum(jnp.where(ids[None, :] < ids[:, None], file_sizes[None, :], 0), axis=1)
    owns = file_writer[None, :] == ids[:, None]
    size_of = jnp.sum(jnp.where(owns, file_sizes[None, :], 0), axis=1)
    wz, wx = ids // SIDE, ids % SIDE
    in_row = (wz[:, None] == wz[None, :]) & (wx[None, :] < wx[:, None])
    in_col = (wx[:, None] == wx[None, :]) & (wz[None, :] < wz[:, None])
    first_row = jnp.sum(jnp.where(in_row, size_of[None, :], 0), axis=1)
    first_col = jnp.sum(jnp.where(in_col, size_of[None, :], 0), axis=1)
    most = jnp.maximum(jnp.max(first_row + size_of), jnp.max(first_col + size_of))
    even = core == 0
    first = jnp.where(even, first_row, first_col)
    f_of, g_of = jnp.where(even, wz, wx), jnp.where(even, wx, wz)

    number = jnp.arange(tensors, dtype=jnp.int32)[:, None]
    inside = (number >= starts[None, :]) & (number < (starts + file_sizes)[None, :])
    first_of_file = jnp.sum(jnp.where(owns, first[:, None], 0), axis=0)
    f_of_file = jnp.sum(jnp.where(owns, f_of[:, None], 0), axis=0)
    line = jnp.sum(jnp.where(inside, f_of_file[None, :], 0), axis=1)
    spot = jnp.sum(jnp.where(inside, (first_of_file - starts)[None, :] + number, 0), axis=1)
    mine = ids == rank
    here = f_of == jnp.sum(jnp.where(mine, f_of, 0))
    at = here[None, :] & (g_of[None, :] == jnp.arange(SIDE, dtype=jnp.int32)[:, None])
    begin = jnp.sum(jnp.where(at, first[None, :], 0), axis=1)
    size = jnp.sum(jnp.where(at, size_of[None, :], 0), axis=1)
    count = jnp.sum(jnp.where(mine, size_of, 0))
    ints = (jnp.concatenate([line, spot]), jnp.concatenate([begin, size]), jnp.stack([count, core]), most)
    return tuple(i.astype(jnp.int32) for i in ints)


def merge_kernel(capacity, place_ref, base_ref, up_ref, down_ref, out_ref, held, held_up, sems):
    tensors = held.shape[0]
    steps = tensors // STEP

    def fetch(step):
        part = pl.ds(step * STEP, STEP)
        yield pltpu.make_async_copy(up_ref.at[part], held_up.at[part], sems.at[0, step])
        yield pltpu.make_async_copy(base_ref.at[part], held.at[part], sems.at[1, step])

    for step in range(steps):
        for copy in fetch(step):
            copy.start()

    @pl.loop(0, steps)
    def _(step):
        for copy in fetch(step):
            copy.wait()
        for i in range(STEP):
            tensor = step * STEP + i
            delta = lax.dot_general(
                held_up[tensor], down_ref[tensor], (((0,), (0,)), ((), ())), preferred_element_type=jnp.float32
            )
            merged = held[tensor].astype(jnp.float32) + scaling * delta
            out_ref[place_ref[tensor] * capacity + place_ref[tensors + tensor]] = merged.astype(jnp.bfloat16)


def merge(place, base, up, down, capacity):
    tensors, rows, cols = base.shape

    def kernel(*refs):
        merge_kernel(capacity, *refs)

    return pl.pallas_call(
        kernel,
        out_shape=jax.ShapeDtypeStruct((SIDE * capacity, rows, cols), jnp.bfloat16),
        in_specs=[
            pl.BlockSpec(memory_space=pltpu.SMEM),
            pl.BlockSpec(memory_space=pl.ANY),
            pl.BlockSpec(memory_space=pl.ANY),
            pl.BlockSpec(memory_space=pltpu.VMEM),
        ],
        out_specs=pl.BlockSpec(memory_space=pltpu.VMEM),
        scratch_shapes=[
            pltpu.VMEM((tensors, rows, cols), jnp.bfloat16),
            pltpu.VMEM((tensors, up.shape[1], rows), jnp.bfloat16),
            pltpu.SemaphoreType.DMA((2, tensors // STEP)),
        ],
        compiler_params=pltpu.CompilerParams(vmem_limit_bytes=2 * VMEM),
        name="merge",
    )(place, base, up, down)


def gather(down_here, row):
    tensors, share, cols = down_here.shape
    y, core = row // 2, row % 2
    whole = jnp.zeros((tensors, 2 * Y, share, cols), down_here.dtype)

    def put(whole, part, k, of_core):
        block = (y + Y - k) % Y * 2 + of_core
        return lax.dynamic_update_slice(whole, part[:, None], (0, block, 0, 0))

    around = {0: down_here}
    for k in (1, 3, 2):
        pairs = [(at * 2 + c, (at + k) % Y * 2 + c) for at in range(Y) for c in range(2)]
        around[k] = lax.ppermute(down_here, "row", pairs)
    for k in (0, 1, 3, 2):
        other = lax.ppermute(around[k], "row", [(at, at ^ 1) for at in range(2 * Y)])
        whole = put(put(whole, around[k], k, core), other, k, 1 - core)
    return whole.reshape(tensors, 2 * Y * share, cols)


def regroup_kernel(lists_ref, arrived_ref, out_ref, sems):
    def each(act):
        for g in range(SIDE):
            begin, size = lists_ref[g], lists_ref[SIDE + g]
            for b, bit in enumerate((8, 4, 2, 1)):

                @pl.when(lax.rem(size, 2 * bit) >= bit)
                def _():
                    before = size - lax.rem(size, 2 * bit)
                    for k in range(SIDE):
                        source = arrived_ref.at[k, pl.ds(begin + before, bit)]
                        act(pltpu.make_async_copy(source, out_ref.at[g, k, pl.ds(before, bit)], sems.at[b, g, k]))

    each(lambda c: c.start())
    each(lambda c: c.wait())


def regroup(lists, arrived):
    side, _, rows, cols = arrived.shape
    return pl.pallas_call(
        regroup_kernel,
        out_shape=jax.ShapeDtypeStruct((side, side, CAP, rows, cols), jnp.bfloat16),
        grid_spec=pltpu.PrefetchScalarGridSpec(
            num_scalar_prefetch=1,
            grid=(1,),
            in_specs=[pl.BlockSpec(memory_space=pl.ANY)],
            out_specs=pl.BlockSpec(memory_space=pl.ANY),
            scratch_shapes=[pltpu.SemaphoreType.DMA((4, side, side))],
        ),
        compiler_params=pltpu.CompilerParams(vmem_limit_bytes=VMEM),
        name="regroup",
    )(lists, arrived)


def unpack_kernel(meta_ref, arrived_ref, out_ref, held, sems):
    count, core = meta_ref[0], meta_ref[1]
    cols = arrived_ref.shape[-1]
    deep = held.shape[0]

    def leave(slot):
        room = lax.rem(slot, deep)
        return pltpu.make_async_copy(held.at[room], out_ref.at[slot], sems.at[room])

    @pl.loop(0, CAP)
    def _(slot):
        room = lax.rem(slot, deep)

        @pl.when(slot >= deep)
        def _():
            leave(slot - deep).wait()

        @pl.when(slot < count)
        def _():
            for g in range(SIDE):
                for f in range(SIDE):
                    source = jnp.where(core == 0, f * SIDE + g, g * SIDE + f)
                    held[room, :, pl.ds(pl.multiple_of(source * cols, cols), cols)] = arrived_ref[g, f, slot]

        @pl.when(slot >= count)
        def _():
            held[room] = jnp.zeros(held.shape[1:], held.dtype)

        leave(slot).start()

    for slot in range(CAP - deep, CAP):
        leave(slot).wait()


def unpack(meta, arrived):
    side, _, slots, rows, cols = arrived.shape
    width = side * side * cols
    return pl.pallas_call(
        unpack_kernel,
        out_shape=jax.ShapeDtypeStruct((slots, rows, width), jnp.bfloat16),
        in_specs=[pl.BlockSpec(memory_space=pltpu.SMEM), pl.BlockSpec(memory_space=pltpu.VMEM)],
        out_specs=pl.BlockSpec(memory_space=pl.ANY),
        scratch_shapes=[pltpu.VMEM((3, rows, width), jnp.bfloat16), pltpu.SemaphoreType.DMA((3,))],
        compiler_params=pltpu.CompilerParams(vmem_limit_bytes=2 * VMEM),
        name="unpack",
    )(meta, arrived)


def to_lines(capacity, place, lists, base, up, down):
    sends = merge(place, base, up, down, capacity)
    arrived = exchange(sends.reshape(SIDE, capacity, *sends.shape[1:]), True)
    return regroup(lists, arrived)


def body(base_weights, adapter_up_factor, adapter_down, file_sizes, file_writer):
    tensors = base_weights.shape[0] * base_weights.shape[1]
    base = base_weights.reshape(tensors, *base_weights.shape[2:])
    up = adapter_up_factor.reshape(tensors, *adapter_up_factor.shape[2:])
    down_here = adapter_down.reshape(tensors, *adapter_down.shape[2:])
    place, lists, meta, most = route(
        file_sizes, file_writer, tensors, lax.axis_index("expert"), lax.axis_index("row") % 2
    )
    which = jnp.sum(most > jnp.array(CAPACITIES[:-1], jnp.int32)).astype(jnp.int32)
    down = gather(down_here, lax.axis_index("row"))
    branches = [lambda *a, c=c: to_lines(c, *a) for c in CAPACITIES]
    groups = lax.switch(which, branches, place, lists, base, up, down)
    groups, meta = lax.optimization_barrier((groups, meta))
    return unpack(meta, exchange(groups, False))


def solution(mesh):
    in_specs = (
        P(None, None, "row", "expert"),
        P(None, None, None, "row"),
        P(None, None, "row", "expert"),
        P(),
        P(),
    )
    out_specs = P("expert", "row", None)
    return jax.shard_map(body, mesh=mesh, in_specs=in_specs, out_specs=out_specs, check_vma=False)
```

```python
import jax
import jax.numpy as jnp
from jax import lax
from jax.experimental import pallas as pl
from jax.experimental.pallas import tpu as pltpu
from jax.sharding import PartitionSpec as P

CAP = 8
SIDE = 4
Y = 4
STEP = 8
CAPACITIES = (18, 20, 21, 22, 23, 24, 25, 26, 28, 32)
scaling = 0.125
VMEM = 16 * 1024 * 1024


def lines(first, rows):
    groups = []
    for row in range(rows):
        along_z = (row % 2 == 0) == first
        for at in range(SIDE):
            ranks = [(i * SIDE + at) if along_z else (at * SIDE + i) for i in range(SIDE)]
            groups.append([rank * rows + row for rank in ranks])
    return groups


def send(block, first, k):
    groups = lines(first, lax.axis_size("row"))
    pairs = [(group[i], group[(i + k) % SIDE]) for group in groups for i in range(SIDE)]
    return lax.ppermute(block, ("expert", "row"), pairs)


def route(file_sizes, file_writer, tensors, rank, core):
    files = file_sizes.shape[0]
    ids = jnp.arange(files, dtype=jnp.int32)
    starts = jnp.sum(jnp.where(ids[None, :] < ids[:, None], file_sizes[None, :], 0), axis=1)
    owns = file_writer[None, :] == ids[:, None]
    size_of = jnp.sum(jnp.where(owns, file_sizes[None, :], 0), axis=1)
    wz, wx = ids // SIDE, ids % SIDE
    in_row = (wz[:, None] == wz[None, :]) & (wx[None, :] < wx[:, None])
    in_col = (wx[:, None] == wx[None, :]) & (wz[None, :] < wz[:, None])
    first_row = jnp.sum(jnp.where(in_row, size_of[None, :], 0), axis=1)
    first_col = jnp.sum(jnp.where(in_col, size_of[None, :], 0), axis=1)
    most = jnp.maximum(jnp.max(first_row + size_of), jnp.max(first_col + size_of))
    even = core == 0
    first = jnp.where(even, first_row, first_col)
    f_of, g_of = jnp.where(even, wz, wx), jnp.where(even, wx, wz)

    number = jnp.arange(tensors, dtype=jnp.int32)[:, None]
    inside = (number >= starts[None, :]) & (number < (starts + file_sizes)[None, :])
    first_of_file = jnp.sum(jnp.where(owns, first[:, None], 0), axis=0)
    f_of_file = jnp.sum(jnp.where(owns, f_of[:, None], 0), axis=0)
    mine = ids == rank
    f_here, g_here = jnp.sum(jnp.where(mine, f_of, 0)), jnp.sum(jnp.where(mine, g_of, 0))
    line = jnp.sum(jnp.where(inside, ((f_of_file + SIDE - f_here) % SIDE)[None, :], 0), axis=1)
    spot = jnp.sum(jnp.where(inside, (first_of_file - starts)[None, :] + number, 0), axis=1)
    further = (g_of + SIDE - g_here) % SIDE
    at = (f_of == f_here)[None, :] & (further[None, :] == jnp.arange(SIDE, dtype=jnp.int32)[:, None])
    begin = jnp.sum(jnp.where(at, first[None, :], 0), axis=1)
    size = jnp.sum(jnp.where(at, size_of[None, :], 0), axis=1)
    count = jnp.sum(jnp.where(mine, size_of, 0))
    ints = (jnp.concatenate([line, spot]), jnp.concatenate([begin, size]), jnp.stack([count, core, f_here, g_here]), most)
    return tuple(i.astype(jnp.int32) for i in ints)


def merge_kernel(capacity, place_ref, base_ref, up_ref, down_ref, out_ref, held, sems):
    tensors = held.shape[0]
    steps = tensors // STEP

    def fetch(step):
        part = pl.ds(step * STEP, STEP)
        return pltpu.make_async_copy(base_ref.at[part], held.at[part], sems.at[step])

    for step in range(steps):
        fetch(step).start()

    @pl.loop(0, steps)
    def _(step):
        fetch(step).wait()
        for i in range(STEP):
            tensor = step * STEP + i
            delta = lax.dot_general(
                up_ref[tensor], down_ref[tensor], (((0,), (0,)), ((), ())), preferred_element_type=jnp.float32
            )
            merged = held[tensor].astype(jnp.float32) + scaling * delta
            out_ref[place_ref[tensor] * capacity + place_ref[tensors + tensor]] = merged.astype(jnp.bfloat16)


def merge(place, base, up, down, capacity):
    tensors, rows, cols = base.shape

    def kernel(*refs):
        merge_kernel(capacity, *refs)

    return pl.pallas_call(
        kernel,
        out_shape=jax.ShapeDtypeStruct((SIDE * capacity, rows, cols), jnp.bfloat16),
        in_specs=[
            pl.BlockSpec(memory_space=pltpu.SMEM),
            pl.BlockSpec(memory_space=pl.ANY),
            pl.BlockSpec(memory_space=pltpu.VMEM),
            pl.BlockSpec(memory_space=pltpu.VMEM),
        ],
        out_specs=pl.BlockSpec(memory_space=pltpu.VMEM),
        scratch_shapes=[
            pltpu.VMEM((tensors, rows, cols), jnp.bfloat16),
            pltpu.SemaphoreType.DMA((tensors // STEP,)),
        ],
        compiler_params=pltpu.CompilerParams(vmem_limit_bytes=2 * VMEM),
        name="merge",
    )(place, base, up, down)


def gather(down_here, row):
    tensors, share, cols = down_here.shape
    y, core = row // 2, row % 2
    whole = jnp.zeros((tensors, 2 * Y, share, cols), down_here.dtype)

    def put(whole, part, k, of_core):
        block = (y + Y - k) % Y * 2 + of_core
        return lax.dynamic_update_slice(whole, part[:, None], (0, block, 0, 0))

    around = {0: down_here}
    for k in (1, 3, 2):
        pairs = [(at * 2 + c, (at + k) % Y * 2 + c) for at in range(Y) for c in range(2)]
        around[k] = lax.ppermute(down_here, "row", pairs)
    for k in (0, 1, 3, 2):
        other = lax.ppermute(around[k], "row", [(at, at ^ 1) for at in range(2 * Y)])
        whole = put(put(whole, around[k], k, core), other, k, 1 - core)
    return whole.reshape(tensors, 2 * Y * share, cols)


def regroup_kernel(ks, lists_ref, *refs):
    blocks, outs, sems = refs[: len(ks)], refs[-1 - SIDE : -1], refs[-1]

    def each(act):
        for r in (2, 1, 3, 0):
            begin, size = lists_ref[r], lists_ref[SIDE + r]
            for b, bit in enumerate((8, 4, 2, 1)):

                @pl.when(lax.rem(size, 2 * bit) >= bit)
                def _():
                    before = size - lax.rem(size, 2 * bit)
                    for i, k in enumerate(ks):
                        source = blocks[i].at[pl.ds(begin + before, bit)]
                        act(pltpu.make_async_copy(source, outs[r].at[k, pl.ds(before, bit)], sems.at[b, r, i]))

    each(lambda c: c.start())
    each(lambda c: c.wait())


def regroup(lists, blocks, ks, before):
    rows, cols = blocks[0].shape[1:]

    def kernel(*refs):
        regroup_kernel(ks, *refs)

    operands = [*blocks, *before]
    return pl.pallas_call(
        kernel,
        out_shape=[jax.ShapeDtypeStruct((SIDE, CAP, rows, cols), jnp.bfloat16)] * SIDE,
        grid_spec=pltpu.PrefetchScalarGridSpec(
            num_scalar_prefetch=1,
            grid=(1,),
            in_specs=[pl.BlockSpec(memory_space=pl.ANY)] * len(operands),
            out_specs=[pl.BlockSpec(memory_space=pl.ANY)] * SIDE,
            scratch_shapes=[pltpu.SemaphoreType.DMA((4, SIDE, len(ks)))],
        ),
        input_output_aliases={1 + len(blocks) + i: i for i in range(len(before))},
        compiler_params=pltpu.CompilerParams(vmem_limit_bytes=VMEM),
        cost_estimate=pl.CostEstimate(
            flops=0, bytes_accessed=4 * len(ks) * SIDE * CAP * rows * cols // 2, transcendentals=0
        ),
        name="regroup",
    )(lists, *operands)


def unpack_kernel(rs, clear, meta_ref, *refs):
    blocks, (out_ref, zeros, sems, zero_sems) = refs[: len(rs)], refs[-4:]
    count, core, f_here, g_here = (meta_ref[i] for i in range(4))
    cols = blocks[0].shape[-1]

    def each(act):
        for b, bit in enumerate((8, 4, 2, 1)):

            @pl.when(lax.rem(count, 2 * bit) >= bit)
            def _():
                slots = pl.ds(count - lax.rem(count, 2 * bit), bit)
                for i, r in enumerate(rs):
                    for k in range(SIDE):
                        f, g = lax.rem(f_here + SIDE - k, SIDE), lax.rem(g_here + SIDE - r, SIDE)
                        source = jnp.where(core == 0, f * SIDE + g, g * SIDE + f)
                        at = pl.ds(pl.multiple_of(source * cols, cols), cols)
                        act(pltpu.make_async_copy(blocks[i].at[k, slots], out_ref.at[slots, :, at], sems.at[b, i, k]))

    def dead(act):
        @pl.loop(count, CAP)
        def _(slot):
            act(pltpu.make_async_copy(zeros, out_ref.at[slot], zero_sems.at[slot]))

    each(lambda c: c.start())
    if clear:
        zeros[...] = jnp.zeros_like(zeros)
        dead(lambda c: c.start())
        dead(lambda c: c.wait())
    each(lambda c: c.wait())


def unpack(meta, blocks, rs, before):
    side, slots, rows, cols = blocks[0].shape
    width = side * side * cols

    def kernel(*refs):
        unpack_kernel(rs, not before, *refs)

    return pl.pallas_call(
        kernel,
        out_shape=jax.ShapeDtypeStruct((slots, rows, width), jnp.bfloat16),
        in_specs=[
            pl.BlockSpec(memory_space=pltpu.SMEM),
            *[pl.BlockSpec(memory_space=pltpu.VMEM)] * len(blocks),
            *[pl.BlockSpec(memory_space=pl.ANY)] * len(before),
        ],
        out_specs=pl.BlockSpec(memory_space=pl.ANY),
        scratch_shapes=[
            pltpu.VMEM((rows, width), jnp.bfloat16),
            pltpu.SemaphoreType.DMA((4, len(rs), side)),
            pltpu.SemaphoreType.DMA((slots,)),
        ],
        input_output_aliases={1 + len(blocks): 0} if before else {},
        compiler_params=pltpu.CompilerParams(vmem_limit_bytes=VMEM),
        cost_estimate=pl.CostEstimate(
            flops=0, bytes_accessed=4 * len(rs) * side * slots * rows * cols, transcendentals=0
        ),
        name="unpack",
    )(meta, *blocks, *before)


def to_lines(capacity, place, lists, base, up, down):
    sends = merge(place, base, up, down, capacity)
    far, right, left = (send(sends[k * capacity : (k + 1) * capacity], True, k) for k in (2, 1, 3))
    groups = regroup(lists, [sends, far], (0, 2), [])
    return regroup(lists, [right, left], (1, 3), groups)


def body(base_weights, adapter_up_factor, adapter_down, file_sizes, file_writer):
    tensors = base_weights.shape[0] * base_weights.shape[1]
    base = base_weights.reshape(tensors, *base_weights.shape[2:])
    up = adapter_up_factor.reshape(tensors, *adapter_up_factor.shape[2:])
    down_here = adapter_down.reshape(tensors, *adapter_down.shape[2:])
    place, lists, meta, most = route(
        file_sizes, file_writer, tensors, lax.axis_index("expert"), lax.axis_index("row") % 2
    )
    which = jnp.sum(most > jnp.array(CAPACITIES[:-1], jnp.int32)).astype(jnp.int32)
    down = gather(down_here, lax.axis_index("row"))
    branches = [lambda *a, c=c: to_lines(c, *a) for c in CAPACITIES]
    groups = lax.switch(which, branches, place, lists, base, up, down)
    far, right, left = (send(groups[r], False, r) for r in (2, 1, 3))
    out = unpack(meta, [groups[0], far], (0, 2), [])
    return unpack(meta, [right, left], (1, 3), [out])


def solution(mesh):
    in_specs = (
        P(None, None, "row", "expert"),
        P(None, None, None, "row"),
        P(None, None, "row", "expert"),
        P(),
        P(),
    )
    out_specs = P("expert", "row", None)
    return jax.shard_map(body, mesh=mesh, in_specs=in_specs, out_specs=out_specs, check_vma=False)
```

```python
import jax
import jax.numpy as jnp
import numpy as np
from jax import lax
from jax.experimental import pallas as pl
from jax.experimental.pallas import tpu as pltpu
from jax.sharding import PartitionSpec as P

CAP = 8
SIDE = 4
Y = 4
STEP = 8
CAPACITIES = (18, 19, 20, 21, 22, 23, 24, 25, 26, 27, 28, 30, 32)
scaling = 0.125
VMEM = 16 * 1024 * 1024


def lines(first, rows):
    groups = []
    for row in range(rows):
        along_z = (row % 2 == 0) == first
        for at in range(SIDE):
            ranks = [(i * SIDE + at) if along_z else (at * SIDE + i) for i in range(SIDE)]
            groups.append([rank * rows + row for rank in ranks])
    return groups


def send(block, first, k):
    groups = lines(first, lax.axis_size("row"))
    pairs = [(group[i], group[(i + k) % SIDE]) for group in groups for i in range(SIDE)]
    return lax.ppermute(block, ("expert", "row"), pairs)


def route(file_sizes, file_writer, tensors, rank, core):
    files = file_sizes.shape[0]
    last, shift = SIDE - 1, SIDE.bit_length() - 1
    ids = np.arange(files, dtype=np.int32)
    wz, wx = ids // SIDE, ids % SIDE
    in_row = (wz[:, None] == wz[None, :]) & (wx[None, :] < wx[:, None])
    in_col = (wx[:, None] == wx[None, :]) & (wz[None, :] < wz[:, None])
    starts = jnp.sum(jnp.where(ids[None, :] < ids[:, None], file_sizes[None, :], 0), axis=1)
    owns = file_writer[None, :] == ids[:, None]
    size_of = jnp.sum(jnp.where(owns, file_sizes[None, :], 0), axis=1)
    first_row = jnp.sum(jnp.where(in_row, size_of[None, :], 0), axis=1)
    first_col = jnp.sum(jnp.where(in_col, size_of[None, :], 0), axis=1)
    most = jnp.maximum(jnp.max(first_row + size_of), jnp.max(first_col + size_of))
    even = core == 0
    first = jnp.where(even, first_row, first_col)
    f_of, g_of = jnp.where(even, wz, wx), jnp.where(even, wx, wz)
    f_here = jnp.where(even, rank >> shift, rank & last)
    g_here = jnp.where(even, rank & last, rank >> shift)

    number = np.arange(tensors, dtype=np.int32)[:, None]
    inside = (number >= starts[None, :]) & (number < (starts + file_sizes)[None, :])
    first_of_file = jnp.sum(jnp.where(owns, first[:, None], 0), axis=0)
    f_of_file = jnp.where(even, file_writer >> shift, file_writer & last)
    line = jnp.sum(jnp.where(inside, ((f_of_file + SIDE - f_here) & last)[None, :], 0), axis=1)
    spot = jnp.sum(jnp.where(inside, (first_of_file - starts)[None, :] + number, 0), axis=1)
    further = (g_of + SIDE - g_here) & last
    at = (f_of == f_here)[None, :] & (further[None, :] == np.arange(SIDE, dtype=np.int32)[:, None])
    begin = jnp.sum(jnp.where(at, first[None, :], 0), axis=1)
    size = jnp.sum(jnp.where(at, size_of[None, :], 0), axis=1)
    count = jnp.sum(jnp.where(ids == rank, size_of, 0))
    ints = (
        jnp.concatenate([line, spot]),
        jnp.concatenate([begin, size]),
        jnp.stack([count, core, f_here, g_here]),
        most,
    )
    return tuple(i.astype(jnp.int32) for i in ints)


def merge_kernel(capacity, place_ref, base_ref, up_ref, down_ref, out_ref, held, sems):
    tensors = held.shape[0]
    steps = tensors // STEP

    def fetch(step):
        part = pl.ds(step * STEP, STEP)
        return pltpu.make_async_copy(base_ref.at[part], held.at[part], sems.at[step])

    for step in range(steps):
        fetch(step).start()

    @pl.loop(0, steps)
    def _(step):
        fetch(step).wait()
        for i in range(STEP):
            tensor = step * STEP + i
            delta = lax.dot_general(
                up_ref[tensor], down_ref[tensor], (((0,), (0,)), ((), ())), preferred_element_type=jnp.float32
            )
            merged = held[tensor].astype(jnp.float32) + scaling * delta
            out_ref[place_ref[tensor] * capacity + place_ref[tensors + tensor]] = merged.astype(jnp.bfloat16)


def merge(place, base, up, down, capacity):
    tensors, rows, cols = base.shape

    def kernel(*refs):
        merge_kernel(capacity, *refs)

    return pl.pallas_call(
        kernel,
        out_shape=jax.ShapeDtypeStruct((SIDE * capacity, rows, cols), jnp.bfloat16),
        in_specs=[
            pl.BlockSpec(memory_space=pltpu.SMEM),
            pl.BlockSpec(memory_space=pl.ANY),
            pl.BlockSpec(memory_space=pltpu.VMEM),
            pl.BlockSpec(memory_space=pltpu.VMEM),
        ],
        out_specs=pl.BlockSpec(memory_space=pltpu.VMEM),
        scratch_shapes=[
            pltpu.VMEM((tensors, rows, cols), jnp.bfloat16),
            pltpu.SemaphoreType.DMA((tensors // STEP,)),
        ],
        compiler_params=pltpu.CompilerParams(vmem_limit_bytes=2 * VMEM),
        name="merge",
    )(place, base, up, down)


def gather(down_here, row):
    tensors, share, cols = down_here.shape
    y, core = row >> 1, row & 1
    whole = jnp.zeros((tensors, 2 * Y, share, cols), down_here.dtype)

    def put(whole, part, k, of_core):
        block = ((y + Y - k) & (Y - 1)) * 2 + of_core
        return lax.dynamic_update_slice(whole, part[:, None], (0, block, 0, 0))

    around = {0: down_here}
    for k in (1, 3, 2):
        pairs = [(at * 2 + c, (at + k) % Y * 2 + c) for at in range(Y) for c in range(2)]
        around[k] = lax.ppermute(down_here, "row", pairs)
    for k in (0, 1, 3, 2):
        other = lax.ppermute(around[k], "row", [(at, at ^ 1) for at in range(2 * Y)])
        whole = put(put(whole, around[k], k, core), other, k, 1 - core)
    return whole.reshape(tensors, 2 * Y * share, cols)


def regroup_kernel(ks, lists_ref, *refs):
    blocks, outs, sems = refs[: len(ks)], refs[-1 - SIDE : -1], refs[-1]

    def each(act):
        for r in (2, 1, 3, 0):
            begin, size = lists_ref[r], lists_ref[SIDE + r]
            for b, bit in enumerate((8, 4, 2, 1)):

                @pl.when(lax.rem(size, 2 * bit) >= bit)
                def _():
                    before = size - lax.rem(size, 2 * bit)
                    for i, k in enumerate(ks):
                        source = blocks[i].at[pl.ds(begin + before, bit)]
                        act(pltpu.make_async_copy(source, outs[r].at[k, pl.ds(before, bit)], sems.at[b, r, i]))

    each(lambda c: c.start())
    each(lambda c: c.wait())


def regroup(lists, blocks, ks, before):
    rows, cols = blocks[0].shape[1:]

    def kernel(*refs):
        regroup_kernel(ks, *refs)

    operands = [*blocks, *before]
    return pl.pallas_call(
        kernel,
        out_shape=[jax.ShapeDtypeStruct((SIDE, CAP, rows, cols), jnp.bfloat16)] * SIDE,
        grid_spec=pltpu.PrefetchScalarGridSpec(
            num_scalar_prefetch=1,
            grid=(1,),
            in_specs=[pl.BlockSpec(memory_space=pl.ANY)] * len(operands),
            out_specs=[pl.BlockSpec(memory_space=pl.ANY)] * SIDE,
            scratch_shapes=[pltpu.SemaphoreType.DMA((4, SIDE, len(ks)))],
        ),
        input_output_aliases={1 + len(blocks) + i: i for i in range(len(before))},
        compiler_params=pltpu.CompilerParams(vmem_limit_bytes=VMEM),
        cost_estimate=pl.CostEstimate(
            flops=0, bytes_accessed=4 * len(ks) * SIDE * CAP * rows * cols // 2, transcendentals=0
        ),
        name="regroup",
    )(lists, *operands)


def unpack_kernel(rs, clear, meta_ref, *refs):
    blocks, (out_ref, zeros, sems, zero_sems) = refs[: len(rs)], refs[-4:]
    count, core, f_here, g_here = (meta_ref[i] for i in range(4))
    cols = blocks[0].shape[-1]

    def each(act):
        for b, bit in enumerate((8, 4, 2, 1)):

            @pl.when(lax.rem(count, 2 * bit) >= bit)
            def _():
                slots = pl.ds(count - lax.rem(count, 2 * bit), bit)
                for i, r in enumerate(rs):
                    for k in range(SIDE):
                        f, g = lax.rem(f_here + SIDE - k, SIDE), lax.rem(g_here + SIDE - r, SIDE)
                        source = jnp.where(core == 0, f * SIDE + g, g * SIDE + f)
                        at = pl.ds(pl.multiple_of(source * cols, cols), cols)
                        act(pltpu.make_async_copy(blocks[i].at[k, slots], out_ref.at[slots, :, at], sems.at[b, i, k]))

    def dead(act):
        @pl.loop(count, CAP)
        def _(slot):
            act(pltpu.make_async_copy(zeros, out_ref.at[slot], zero_sems.at[slot]))

    each(lambda c: c.start())
    if clear:
        zeros[...] = jnp.zeros_like(zeros)
        dead(lambda c: c.start())
        dead(lambda c: c.wait())
    each(lambda c: c.wait())


def unpack(meta, blocks, rs, before):
    side, slots, rows, cols = blocks[0].shape
    width = side * side * cols

    def kernel(*refs):
        unpack_kernel(rs, not before, *refs)

    return pl.pallas_call(
        kernel,
        out_shape=jax.ShapeDtypeStruct((slots, rows, width), jnp.bfloat16),
        in_specs=[
            pl.BlockSpec(memory_space=pltpu.SMEM),
            *[pl.BlockSpec(memory_space=pltpu.VMEM)] * len(blocks),
            *[pl.BlockSpec(memory_space=pl.ANY)] * len(before),
        ],
        out_specs=pl.BlockSpec(memory_space=pl.ANY),
        scratch_shapes=[
            pltpu.VMEM((rows, width), jnp.bfloat16),
            pltpu.SemaphoreType.DMA((4, len(rs), side)),
            pltpu.SemaphoreType.DMA((slots,)),
        ],
        input_output_aliases={1 + len(blocks): 0} if before else {},
        compiler_params=pltpu.CompilerParams(vmem_limit_bytes=VMEM),
        cost_estimate=pl.CostEstimate(
            flops=0, bytes_accessed=4 * len(rs) * side * slots * rows * cols, transcendentals=0
        ),
        name="unpack",
    )(meta, *blocks, *before)


def to_lines(capacity, place, lists, base, up, down):
    sends = merge(place, base, up, down, capacity)
    far, right, left = (send(sends[k * capacity : (k + 1) * capacity], True, k) for k in (2, 1, 3))
    groups = regroup(lists, [sends, far], (0, 2), [])
    return regroup(lists, [right, left], (1, 3), groups)


def body(base_weights, adapter_up_factor, adapter_down, file_sizes, file_writer):
    tensors = base_weights.shape[0] * base_weights.shape[1]
    base = base_weights.reshape(tensors, *base_weights.shape[2:])
    up = adapter_up_factor.reshape(tensors, *adapter_up_factor.shape[2:])
    down_here = adapter_down.reshape(tensors, *adapter_down.shape[2:])
    place, lists, meta, most = route(
        file_sizes, file_writer, tensors, lax.axis_index("expert"), lax.axis_index("row") & 1
    )
    which = jnp.sum(most > jnp.array(CAPACITIES[:-1], jnp.int32)).astype(jnp.int32)
    down = gather(down_here, lax.axis_index("row"))
    branches = [lambda *a, c=c: to_lines(c, *a) for c in CAPACITIES]
    groups = lax.switch(which, branches, place, lists, base, up, down)
    far, right, left = (send(groups[r], False, r) for r in (2, 1, 3))
    out = unpack(meta, [groups[0], far], (0, 2), [])
    return unpack(meta, [right, left], (1, 3), [out])


def solution(mesh):
    in_specs = (
        P(None, None, "row", "expert"),
        P(None, None, None, "row"),
        P(None, None, "row", "expert"),
        P(),
        P(),
    )
    out_specs = P("expert", "row", None)
    return jax.shard_map(body, mesh=mesh, in_specs=in_specs, out_specs=out_specs, check_vma=False)
```

```python
import jax
import jax.numpy as jnp
import numpy as np
from jax import lax
from jax.experimental import pallas as pl
from jax.experimental.pallas import tpu as pltpu
from jax.sharding import PartitionSpec as P

CAP = 8
SIDE = 4
Y = 4
STEP = 8
CAPACITIES = (18, 19, 20, 21, 22, 23, 24, 25, 26, 27, 28, 30, 32)
scaling = 0.125
VMEM = 16 * 1024 * 1024


def lines(first, rows):
    groups = []
    for row in range(rows):
        along_z = (row % 2 == 0) == first
        for at in range(SIDE):
            ranks = [(i * SIDE + at) if along_z else (at * SIDE + i) for i in range(SIDE)]
            groups.append([rank * rows + row for rank in ranks])
    return groups


def send(block, first, k):
    groups = lines(first, lax.axis_size("row"))
    pairs = [(group[i], group[(i + k) % SIDE]) for group in groups for i in range(SIDE)]
    return lax.ppermute(block, ("expert", "row"), pairs)


def route(file_sizes, file_writer, sizes_late, writer_late, tensors, rank, core):
    files = file_sizes.shape[0]
    last, shift = SIDE - 1, SIDE.bit_length() - 1
    ids = np.arange(files, dtype=np.int32)
    wz, wx = ids // SIDE, ids % SIDE
    in_row = (wz[:, None] == wz[None, :]) & (wx[None, :] < wx[:, None])
    in_col = (wx[:, None] == wx[None, :]) & (wz[None, :] < wz[:, None])
    starts = jnp.sum(jnp.where(ids[None, :] < ids[:, None], file_sizes[None, :], 0), axis=1)
    owns = file_writer[None, :] == ids[:, None]
    size_of = jnp.sum(jnp.where(owns, file_sizes[None, :], 0), axis=1)
    first_row = jnp.sum(jnp.where(in_row, size_of[None, :], 0), axis=1)
    first_col = jnp.sum(jnp.where(in_col, size_of[None, :], 0), axis=1)
    most = jnp.maximum(jnp.max(first_row + size_of), jnp.max(first_col + size_of))
    even = core == 0
    first = jnp.where(even, first_row, first_col)
    f_of, g_of = jnp.where(even, wz, wx), jnp.where(even, wx, wz)
    f_here = jnp.where(even, rank >> shift, rank & last)
    g_here = jnp.where(even, rank & last, rank >> shift)

    number = np.arange(tensors, dtype=np.int32)[:, None]
    inside = (number >= starts[None, :]) & (number < (starts + sizes_late)[None, :])
    first_of_file = jnp.sum(jnp.where(owns, first[:, None], 0), axis=0)
    f_of_file = jnp.where(even, writer_late >> shift, writer_late & last)
    line = jnp.sum(jnp.where(inside, ((f_of_file + SIDE - f_here) & last)[None, :], 0), axis=1)
    spot = jnp.sum(jnp.where(inside, (first_of_file - starts)[None, :] + number, 0), axis=1)
    further = (g_of + SIDE - g_here) & last
    at = (f_of == f_here)[None, :] & (further[None, :] == np.arange(SIDE, dtype=np.int32)[:, None])
    begin = jnp.sum(jnp.where(at, first[None, :], 0), axis=1)
    size = jnp.sum(jnp.where(at, size_of[None, :], 0), axis=1)
    count = jnp.sum(jnp.where(ids == rank, size_of, 0))
    ints = (
        jnp.concatenate([line, spot]),
        jnp.concatenate([begin, size]),
        jnp.stack([count, core, f_here, g_here]),
        most,
    )
    return tuple(i.astype(jnp.int32) for i in ints)


def merge_kernel(capacity, place_ref, base_ref, up_ref, down_ref, out_ref, held, sems):
    tensors = held.shape[0]
    steps = tensors // STEP

    def fetch(step):
        part = pl.ds(step * STEP, STEP)
        return pltpu.make_async_copy(base_ref.at[part], held.at[part], sems.at[step])

    for step in range(steps):
        fetch(step).start()

    @pl.loop(0, steps)
    def _(step):
        fetch(step).wait()
        for i in range(STEP):
            tensor = step * STEP + i
            delta = lax.dot_general(
                up_ref[tensor], down_ref[tensor], (((0,), (0,)), ((), ())), preferred_element_type=jnp.float32
            )
            merged = held[tensor].astype(jnp.float32) + scaling * delta
            out_ref[place_ref[tensor] * capacity + place_ref[tensors + tensor]] = merged.astype(jnp.bfloat16)


def merge(place, base, up, down, capacity):
    tensors, rows, cols = base.shape

    def kernel(*refs):
        merge_kernel(capacity, *refs)

    return pl.pallas_call(
        kernel,
        out_shape=jax.ShapeDtypeStruct((SIDE * capacity, rows, cols), jnp.bfloat16),
        in_specs=[
            pl.BlockSpec(memory_space=pltpu.SMEM),
            pl.BlockSpec(memory_space=pl.ANY),
            pl.BlockSpec(memory_space=pltpu.VMEM),
            pl.BlockSpec(memory_space=pltpu.VMEM),
        ],
        out_specs=pl.BlockSpec(memory_space=pltpu.VMEM),
        scratch_shapes=[
            pltpu.VMEM((tensors, rows, cols), jnp.bfloat16),
            pltpu.SemaphoreType.DMA((tensors // STEP,)),
        ],
        compiler_params=pltpu.CompilerParams(vmem_limit_bytes=2 * VMEM),
        name="merge",
    )(place, base, up, down)


def gather_y(down_here):
    around = {0: down_here}
    for k in (1, 3, 2):
        pairs = [(at * 2 + c, (at + k) % Y * 2 + c) for at in range(Y) for c in range(2)]
        around[k] = lax.ppermute(down_here, "row", pairs)
    return around


def gather_core(around, row):
    tensors, share, cols = around[0].shape
    y, core = row >> 1, row & 1
    whole = jnp.zeros((tensors, 2 * Y, share, cols), around[0].dtype)

    def put(whole, part, k, of_core):
        block = ((y + Y - k) & (Y - 1)) * 2 + of_core
        return lax.dynamic_update_slice(whole, part[:, None], (0, block, 0, 0))

    for k in (1, 3, 2, 0):
        other = lax.ppermute(around[k], "row", [(at, at ^ 1) for at in range(2 * Y)])
        whole = put(put(whole, around[k], k, core), other, k, 1 - core)
    return whole.reshape(tensors, 2 * Y * share, cols)


def regroup_kernel(ks, lists_ref, *refs):
    blocks, outs, sems = refs[: len(ks)], refs[-1 - SIDE : -1], refs[-1]

    def each(act):
        for r in (2, 1, 3, 0):
            begin, size = lists_ref[r], lists_ref[SIDE + r]
            for b, bit in enumerate((8, 4, 2, 1)):

                @pl.when(lax.rem(size, 2 * bit) >= bit)
                def _():
                    before = size - lax.rem(size, 2 * bit)
                    for i, k in enumerate(ks):
                        source = blocks[i].at[pl.ds(begin + before, bit)]
                        act(pltpu.make_async_copy(source, outs[r].at[k, pl.ds(before, bit)], sems.at[b, r, i]))

    each(lambda c: c.start())
    each(lambda c: c.wait())


def regroup(lists, blocks, ks, before):
    rows, cols = blocks[0].shape[1:]

    def kernel(*refs):
        regroup_kernel(ks, *refs)

    operands = [*blocks, *before]
    return pl.pallas_call(
        kernel,
        out_shape=[jax.ShapeDtypeStruct((SIDE, CAP, rows, cols), jnp.bfloat16)] * SIDE,
        grid_spec=pltpu.PrefetchScalarGridSpec(
            num_scalar_prefetch=1,
            grid=(1,),
            in_specs=[pl.BlockSpec(memory_space=pl.ANY)] * len(operands),
            out_specs=[pl.BlockSpec(memory_space=pl.ANY)] * SIDE,
            scratch_shapes=[pltpu.SemaphoreType.DMA((4, SIDE, len(ks)))],
        ),
        input_output_aliases={1 + len(blocks) + i: i for i in range(len(before))},
        compiler_params=pltpu.CompilerParams(vmem_limit_bytes=VMEM),
        cost_estimate=pl.CostEstimate(
            flops=0, bytes_accessed=4 * len(ks) * SIDE * CAP * rows * cols // 2, transcendentals=0
        ),
        name="regroup",
    )(lists, *operands)


def unpack_kernel(rs, clear, meta_ref, *refs):
    blocks, (out_ref, zeros, sems, zero_sems) = refs[: len(rs)], refs[-4:]
    count, core, f_here, g_here = (meta_ref[i] for i in range(4))
    cols = blocks[0].shape[-1]

    def each(act):
        for b, bit in enumerate((8, 4, 2, 1)):

            @pl.when(lax.rem(count, 2 * bit) >= bit)
            def _():
                slots = pl.ds(count - lax.rem(count, 2 * bit), bit)
                for i, r in enumerate(rs):
                    for k in range(SIDE):
                        f, g = lax.rem(f_here + SIDE - k, SIDE), lax.rem(g_here + SIDE - r, SIDE)
                        source = jnp.where(core == 0, f * SIDE + g, g * SIDE + f)
                        at = pl.ds(pl.multiple_of(source * cols, cols), cols)
                        act(pltpu.make_async_copy(blocks[i].at[k, slots], out_ref.at[slots, :, at], sems.at[b, i, k]))

    def dead(act):
        @pl.loop(count, CAP)
        def _(slot):
            act(pltpu.make_async_copy(zeros, out_ref.at[slot], zero_sems.at[slot]))

    each(lambda c: c.start())
    if clear:
        zeros[...] = jnp.zeros_like(zeros)
        dead(lambda c: c.start())
        dead(lambda c: c.wait())
    each(lambda c: c.wait())


def unpack(meta, blocks, rs, before):
    side, slots, rows, cols = blocks[0].shape
    width = side * side * cols

    def kernel(*refs):
        unpack_kernel(rs, not before, *refs)

    return pl.pallas_call(
        kernel,
        out_shape=jax.ShapeDtypeStruct((slots, rows, width), jnp.bfloat16),
        in_specs=[
            pl.BlockSpec(memory_space=pltpu.SMEM),
            *[pl.BlockSpec(memory_space=pltpu.VMEM)] * len(blocks),
            *[pl.BlockSpec(memory_space=pl.ANY)] * len(before),
        ],
        out_specs=pl.BlockSpec(memory_space=pl.ANY),
        scratch_shapes=[
            pltpu.VMEM((rows, width), jnp.bfloat16),
            pltpu.SemaphoreType.DMA((4, len(rs), side)),
            pltpu.SemaphoreType.DMA((slots,)),
        ],
        input_output_aliases={1 + len(blocks): 0} if before else {},
        compiler_params=pltpu.CompilerParams(vmem_limit_bytes=VMEM),
        cost_estimate=pl.CostEstimate(
            flops=0, bytes_accessed=4 * len(rs) * side * slots * rows * cols, transcendentals=0
        ),
        name="unpack",
    )(meta, *blocks, *before)


def to_lines(capacity, place, lists, base, up, down):
    sends = merge(place, base, up, down, capacity)
    far, right, left = (send(sends[k * capacity : (k + 1) * capacity], True, k) for k in (2, 1, 3))
    groups = regroup(lists, [sends, far], (0, 2), [])
    return regroup(lists, [right, left], (1, 3), groups)


def body(base_weights, adapter_up_factor, adapter_down, file_sizes, file_writer):
    tensors = base_weights.shape[0] * base_weights.shape[1]
    base = base_weights.reshape(tensors, *base_weights.shape[2:])
    up = adapter_up_factor.reshape(tensors, *adapter_up_factor.shape[2:])
    down_here = adapter_down.reshape(tensors, *adapter_down.shape[2:])
    around, sizes_late, writer_late = lax.optimization_barrier((gather_y(down_here), file_sizes, file_writer))
    place, lists, meta, most = route(
        file_sizes, file_writer, sizes_late, writer_late, tensors, lax.axis_index("expert"), lax.axis_index("row") & 1
    )
    which = jnp.sum(most > jnp.array(CAPACITIES[:-1], jnp.int32)).astype(jnp.int32)
    down = gather_core(around, lax.axis_index("row"))
    branches = [lambda *a, c=c: to_lines(c, *a) for c in CAPACITIES]
    groups = lax.switch(which, branches, place, lists, base, up, down)
    far, right, left = (send(groups[r], False, r) for r in (2, 1, 3))
    out = unpack(meta, [groups[0], far], (0, 2), [])
    return unpack(meta, [right, left], (1, 3), [out])


def solution(mesh):
    in_specs = (
        P(None, None, "row", "expert"),
        P(None, None, None, "row"),
        P(None, None, "row", "expert"),
        P(),
        P(),
    )
    out_specs = P("expert", "row", None)
    return jax.shard_map(body, mesh=mesh, in_specs=in_specs, out_specs=out_specs, check_vma=False)
```
